512 devices in a mesh: elem: 128 (over x, z, core), blk: 4 (over y).
Axes of the slice: x: 4, y: 4, z: 16, core: 2. Of those that a mesh axis runs over, the one named last changes fastest.
Arguments:
- diagonal_block_list: bfloat16 [512, 512, 512], P('elem', None, 'blk'), may hold values from -0.25 to 0.25
- neighbour_block_list: bfloat16 [512, 6, 512, 512], P('elem', None, None, 'blk'), may hold values from -0.25 to 0.25
- neighbours: int32 [512, 6], P('elem'), may hold values from 0 to 511, as said below
- damping: float32 [512, 512], P('elem', 'blk'), may hold values from 0.05 to 0.3
- bases: bfloat16 [512, 512, 128], P('elem', 'blk'), may hold values from -1.1953125 to 1.1953125
- agglomerate: int32 [512], replicated, may hold values from 0 to 255, as said below
- group: int32 [256], replicated, may hold values from 0 to 7
Outputs:
- smoothed: bfloat16 [512, 512, 128], P('elem', 'blk')
- coarse: float32 [256, 128, 128], P('elem', 'blk')
- last_level: float32 [8, 128, 128], P(None, 'blk')
The draws below stay inside these ranges and needn't reach their ends.
Inputs may be any that keep to these rules, and one draw needn't show every extreme that they name: `neighbours`: each neighbour lies on the same index of elem as its element or on the next index on either side; every index of elem has a neighbour on an adjacent index. The elements of one agglomerate are consecutive; every agglomerate has one element or more.
All inputs are finite; a program needn't handle non-finite values.
Results may differ from the reference program's by a relative error of at most 0.007.
Values may be sent and summed in bfloat16 or wider, within the bound.
A program may use at most 64 MiB of HBM per device.

```python
import math
import jax
import jax.numpy as jnp
from jax import lax

NB = 512
NC = 128
NBR = 6
SWEEPS = 2
NG = 8
E_DEV = 4
NE = 512
NAGG = 256
N_ELEM = 128


def draw_neighbours(key, part):
    key_side = jax.random.fold_in(key, 11)
    key_local = jax.random.fold_in(key, 12)
    element = jnp.arange(NE, dtype=jnp.int32)
    device = element // E_DEV
    offset = jax.random.randint(key_side, (NE, NBR), -1, 2)
    target = jnp.clip(device[:, None] + offset, 0, N_ELEM - 1)
    forced = jnp.where(device + 1 < N_ELEM, device + 1, device - 1)
    is_first = (element % E_DEV == 0)[:, None] & (jnp.arange(NBR)[None, :] == 0)
    target = jnp.where(is_first, forced[:, None], target)
    local_index = jax.random.randint(key_local, (NE, NBR), 0, E_DEV)
    return (target * E_DEV + local_index).astype(jnp.int32)


def draw_agglomerate(key, part):
    key_cuts = jax.random.fold_in(key, 21)
    key_names = jax.random.fold_in(key, 22)
    cuts = jax.random.permutation(key_cuts, NE - 1)[:NAGG - 1] + 1
    starts = jnp.zeros((NE,), jnp.int32).at[cuts].set(1)
    run_index = jnp.cumsum(starts).astype(jnp.int32)
    labels = jax.random.permutation(key_names, NAGG).astype(jnp.int32)
    return jnp.take(labels, run_index, axis=0).astype(jnp.int32)


def touch_ends(values, key, least, largest):
    place = [jax.random.randint(jax.random.fold_in(key, axis), (), 0, length) for axis, length in enumerate(values.shape)]
    longest = values.shape.index(max(values.shape))
    neighbour = place[:longest] + [(place[longest] + 1) % values.shape[longest]] + place[longest + 1:]
    return values.at[tuple(place)].set(least).at[tuple(neighbour)].set(largest)


def shard_levels(key, shape, shards, low, largest):
    factor_of = 1.0
    for axis_at, shards_of in shards:
        draws = jax.random.uniform(jax.random.fold_in(jax.random.fold_in(key, 6), axis_at), (shards_of,), jnp.float32, low / len(shards), largest / len(shards))
        factor_of = factor_of * jnp.repeat(jnp.exp(draws), shape[axis_at] // shards_of).reshape((-1,) + (1,) * (len(shape) - 1 - axis_at))
    return factor_of


def noise(stream_key, dims, width, reach, split=(), held_as=jnp.bfloat16):
    array = jax.random.normal(stream_key, dims, jnp.float32) * width
    if len(split) > 0:
        array = shard_levels(stream_key, dims, split, -0.22, 0.18) * array
    return jnp.clip(array, min=-reach, max=reach).astype(held_as)


def setup_inputs(seed: int = 0) -> dict:
    key_of = jax.random.split(jax.random.key(seed), 8)
    diagonal_block_list = noise(key_of[0], (NE, NB, NB), NB ** -0.5, 0.25, ((0, 128), (2, 4)))
    neighbour_block_list = noise(key_of[1], (NE, NBR, NB, NB), NB ** -0.5, 0.25, ((0, 128), (3, 4)))
    neighbours = draw_neighbours(jax.random.fold_in(key_of[7], 71), 0)
    damping = jnp.clip(jnp.exp(math.log(0.3) - 1.7917595 * jax.random.uniform(key_of[3], (NE, NB), jnp.float32) ** shard_levels(key_of[3], (NE, NB), ((0, 128), (1, 4)), -0.2, 0.2)), 0.05, 0.3)
    bases = noise(key_of[4], (NE, NB, NC), 0.2, 1.1953125, ((0, 128), (1, 4)))
    agglomerate = draw_agglomerate(jax.random.fold_in(key_of[7], 71), 0)
    group = touch_ends(jax.random.randint(key_of[6], (NAGG,), 0, NG), jax.random.fold_in(key_of[6], 1), 0, NG - 1).astype(jnp.int32)
    return dict(diagonal_block_list=diagonal_block_list, neighbour_block_list=neighbour_block_list, neighbours=neighbours, damping=damping, bases=bases, agglomerate=agglomerate, group=group)


def smooth_pass(source, diagonal_block_list, neighbour_block_list, neighbours, damping):
    def smooth_one(item):
        diag_part, nbr_part, neighbour_ids, own_rows, damp_rows = item
        nearby_elements = jnp.take(source, neighbour_ids, axis=0)
        total_result = jnp.dot(diag_part, own_rows, preferred_element_type=jnp.float32)
        total_result = total_result + jnp.einsum("kij,kjc->ic", nbr_part.astype(jnp.float32), nearby_elements.astype(jnp.float32))
        return (own_rows.astype(jnp.float32) - damp_rows[:, None] * total_result).astype(jnp.bfloat16)
    return lax.map(smooth_one, (diagonal_block_list, neighbour_block_list, neighbours, source, damping))


def reference(diagonal_block_list, neighbour_block_list, neighbours, damping, bases, agglomerate, group):
    present_value = bases
    for sweep_index in range(SWEEPS):
        present_value = smooth_pass(present_value, diagonal_block_list, neighbour_block_list, neighbours, damping)
    smoothed = present_value
    elem_group = jnp.take(group, agglomerate, axis=0)

    def couple_one(item):
        diag_part, nbr_part, neighbour_ids, own_rows, own_cluster, own_group = item
        left_diag = jnp.dot(own_rows.T, diag_part, preferred_element_type=jnp.float32).astype(jnp.bfloat16)
        left_nbr = jnp.einsum("ic,kis->kcs", own_rows.astype(jnp.float32), nbr_part.astype(jnp.float32)).astype(jnp.bfloat16)
        self_term = jnp.dot(left_diag, own_rows, preferred_element_type=jnp.float32)
        nearby_elements = jnp.take(smoothed, neighbour_ids, axis=0)
        nbr_terms = jnp.einsum("kcs,ksd->kcd", left_nbr.astype(jnp.float32), nearby_elements.astype(jnp.float32))
        same_cluster = (jnp.take(agglomerate, neighbour_ids, axis=0) == own_cluster).astype(jnp.float32)
        same_group = (jnp.take(elem_group, neighbour_ids, axis=0) == own_group).astype(jnp.float32)
        first_sum = self_term + jnp.sum(same_cluster[:, None, None] * nbr_terms, 0)
        second_level_sum = self_term + jnp.sum(same_group[:, None, None] * nbr_terms, 0)
        return first_sum, second_level_sum

    first_all, second_all = lax.map(couple_one, (diagonal_block_list, neighbour_block_list, neighbours, smoothed, agglomerate, elem_group))
    coarse = jax.ops.segment_sum(first_all, agglomerate, num_segments=NAGG)
    last_level = jax.ops.segment_sum(second_all, elem_group, num_segments=NG)
    return smoothed, coarse, last_level
```

```python
import functools

import jax
import jax.numpy as jnp
from jax import lax
from jax.experimental import pallas as pl
from jax.experimental.pallas import tpu as pltpu
from jax.sharding import PartitionSpec as P

MESH = pl.DeviceIdType.MESH
F32 = jnp.float32
BF16 = jnp.bfloat16
NL = 4
NBR = 6
BLK = 4
NX = 4
NC = 128
RB = 128
ROWS = RB * BLK
KK = (NBR + 1) * RB
HR = NC // BLK
SWEEPS = 2


def remote(src, dst, send_sem, recv_sem, device):
    return pltpu.make_async_remote_copy(
        src_ref=src,
        dst_ref=dst,
        send_sem=send_sem,
        recv_sem=recv_sem,
        device_id=device,
        device_id_type=MESH,
    )


def kernel(
    nz,
    nbr_s,
    agg_s,
    grp_s,
    damp_ref,
    diag_hbm,
    nbrs_hbm,
    bases_hbm,
    smooth_ref,
    coarse_ref,
    last_ref,
    a_v,
    xe0,
    xe1,
    xe2,
    xg,
    xg2,
    dmp,
    ysum,
    y_opp,
    y_plain,
    y_relay,
    y_r1,
    y_rp,
    y_rr,
    xa,
    zs,
    gsum,
    g_opp,
    g_plain,
    g_relay,
    g_r1,
    g_rp,
    g_rr,
    gx,
    c8h,
    hs,
    hx,
    km,
    pb,
    rz,
    l1,
    l2,
    ll,
    a_sem,
    b_sem,
    halo_ss,
    halo_rs,
    y_ss,
    y_rs,
    ag_ss,
    ag_rs,
    d_ss,
    d_rs,
    x_ss,
    x_rs,
    z_ss,
    z_rs,
    l1_ss,
    l1_rs,
    l2_ss,
    l2_rs,
    f_ss,
    f_rs,
):
    xe = (xe0, xe1, xe2)
    ne = nz * NX * 2
    zl_n = min(4, nz)
    zh_n = nz // zl_n
    me = lax.axis_index("elem")
    b = lax.axis_index("blk")
    core = lax.rem(me, 2)
    zc = lax.rem(me // 2, nz)
    xc = me // (2 * nz)
    rt = lax.rem(b + 1, BLK)
    op = lax.rem(b + 2, BLK)
    lt = lax.rem(b + 3, BLK)
    nxt = (lax.rem(me + 1, ne), b)
    prv = (lax.rem(me + ne - 1, ne), b)
    right, left = (me, rt), (me, lt)

    def at(x, z, c):
        return ((x * nz + z) * 2 + c, b)

    line = []
    for dx in range(NX):
        for dc in range(2):
            if dx or dc:
                line.append(at(lax.rem(xc + dx, NX), zc, lax.rem(core + dc, 2)))

    barrier = pltpu.get_barrier_semaphore()
    partners = [nxt, prv, right, left, *line]
    for dev in partners:
        pl.semaphore_signal(barrier, inc=1, device_id=dev, device_id_type=MESH)

    def greet(dz, carry):
        pl.semaphore_signal(
            barrier,
            inc=1,
            device_id=at(xc, lax.rem(zc + dz, nz), core),
            device_id_type=MESH,
        )
        return carry

    lax.fori_loop(1, nz, greet, 0)

    own_in = pltpu.make_async_copy(bases_hbm, xe[0].at[pl.ds(NL, NL)], b_sem)
    own_in.start()

    def load_a(e, carry):
        pltpu.make_async_copy(
            diag_hbm.at[e], a_v.at[e, :, pl.ds(0, RB)], a_sem.at[e]
        ).start()
        for k in range(NBR):
            pltpu.make_async_copy(
                nbrs_hbm.at[e, k],
                a_v.at[e, :, pl.ds((k + 1) * RB, RB)],
                a_sem.at[e],
            ).start()
        return carry

    lax.fori_loop(0, NL, load_a, 0)

    pl.semaphore_wait(barrier, len(partners) + nz - 1)

    h0n = remote(bases_hbm, xe[0].at[pl.ds(0, NL)], halo_ss.at[0, 0, 0], halo_rs.at[0, 0, 0], nxt)
    h0p = remote(
        bases_hbm, xe[0].at[pl.ds(2 * NL, NL)], halo_ss.at[0, 1, 0], halo_rs.at[0, 1, 0], prv
    )
    h0n.start()
    h0p.start()

    for e in range(NL):
        dmp[e] = jnp.broadcast_to(damp_ref[pl.ds(e, 1), :], (RB, NC)).T

    lane = lax.broadcasted_iota(jnp.int32, (16, 512), 1)
    row = lax.broadcasted_iota(jnp.int32, (16, 512), 0)

    def place(i, slots):
        xx, cc, j = i // 8, lax.rem(i // 4, 2), lax.rem(i, 4)
        a = agg_s[((xx * nz + zc) * 2 + cc) * NL + j]
        dev = a // 2
        mine = (lax.rem(dev, 2) == core) & (dev // (2 * nz) == xc)
        slot = jnp.where(mine, lax.rem(dev // 2, nz) * 2 + lax.rem(a, 2), -1)
        return jnp.where(lane // 16 == i, slot, slots)

    slots = lax.fori_loop(0, 32, place, jnp.full((16, 512), -1, jnp.int32))
    same_row = row == lax.rem(lane, 16)

    def fill(s, carry):
        km[pl.ds(pl.multiple_of(s * 16, 16), 16), :] = jnp.where(
            (slots == s) & same_row, 1.0, 0.0
        ).astype(BF16)
        return carry

    lax.fori_loop(0, 2 * nz, fill, 0)

    own_in.wait()
    h0n.wait_recv()
    h0p.wait_recv()

    first = (me - 1) * NL

    def nearby(e, k):
        return jnp.clip(nbr_s[e, k] - first, 0, 3 * NL - 1)

    def wait_a(e):
        pltpu.make_async_copy(a_v.at[e], a_v.at[e], a_sem.at[e]).wait()

    def sides(to_right):
        if to_right:
            return right, rt, left, lt
        return left, lt, right, rt

    def opp_copy(st, e, bufs, to_right):
        near = sides(to_right)[0]
        return remote(bufs[1].at[e], bufs[4].at[e], y_ss.at[st, 0, e], y_rs.at[st, 0, e], near)

    def plain_copy(st, e, bufs, to_right):
        far = sides(to_right)[2]
        return remote(bufs[2].at[e], bufs[5].at[e], y_ss.at[st, 1, e], y_rs.at[st, 1, e], far)

    def relay_copy(st, e, bufs, to_right):
        near = sides(to_right)[0]
        return remote(bufs[3].at[e], bufs[6].at[e], y_ss.at[st, 2, e], y_rs.at[st, 2, e], near)

    def reduce_send(st, e, bufs, to_right):
        total, opp, plain = bufs[:3]
        opp[e] = total[e, op].astype(BF16)
        opp_copy(st, e, bufs, to_right).start()
        plain[e] = total[e, sides(to_right)[3]].astype(BF16)
        plain_copy(st, e, bufs, to_right).start()

    def reduce_relay(st, e, bufs, to_right):
        opp_copy(st, e, bufs, to_right).wait_recv()
        bufs[3][e] = (bufs[0][e, sides(to_right)[1]] + bufs[4][e].astype(F32)).astype(BF16)
        relay_copy(st, e, bufs, to_right).start()

    def reduced(st, e, bufs, to_right):
        plain_copy(st, e, bufs, to_right).wait_recv()
        relay_copy(st, e, bufs, to_right).wait_recv()
        return bufs[0][e, b] + bufs[5][e].astype(F32) + bufs[6][e].astype(F32)

    def reduce_drain(st, bufs):
        def drain(i, carry):
            for e, to_right in ((i, True), (i + 2, False)):
                opp_copy(st, e, bufs, to_right).wait_send()
                plain_copy(st, e, bufs, to_right).wait_send()
                relay_copy(st, e, bufs, to_right).wait_send()
            return carry

        lax.fori_loop(0, 2, drain, 0)

    def pairs(step):
        def one(i, carry):
            step(i, True)
            step(i + 2, False)
            return carry

        lax.fori_loop(0, 2, one, 0)

    def halo_next(st, e):
        return remote(
            xe[st].at[NL + e], xe[st].at[e], halo_ss.at[st, 0, e], halo_rs.at[st, 0, e], nxt
        )

    def halo_prev(st, e):
        return remote(
            xe[st].at[NL + e], xe[st].at[2 * NL + e], halo_ss.at[st, 1, e], halo_rs.at[st, 1, e], prv
        )

    def gather_right(e, owner):
        return remote(
            xe[SWEEPS].at[NL + e], xa.at[e, owner], ag_ss.at[0, e], ag_rs.at[0, e], right
        )

    def gather_left(e, owner):
        return remote(
            xe[SWEEPS].at[NL + e], xa.at[e, owner], ag_ss.at[1, e], ag_rs.at[1, e], left
        )

    def gather_on(e, to_right, owner):
        near = sides(to_right)[0]
        return remote(xa.at[e, owner], xa.at[e, owner], ag_ss.at[2, e], ag_rs.at[2, e], near)

    for s in range(SWEEPS):
        bufs = (
            ysum,
            y_opp.at[s],
            y_plain.at[s],
            y_relay.at[s],
            y_r1.at[s],
            y_rp.at[s],
            y_rr.at[s],
        )

        def product(e, to_right, s=s, bufs=bufs):
            if s == 0:
                wait_a(e)
            xg[pl.ds(0, RB), :] = xe[s][NL + e]
            for k in range(NBR):
                xg[pl.ds((k + 1) * RB, RB), :] = xe[s][nearby(e, k)]
            y = jnp.dot(a_v[e], xg[...], preferred_element_type=F32)
            ysum[e] = y.reshape(BLK, RB, NC)
            reduce_send(s, e, bufs, to_right)

        pairs(product)
        pairs(functools.partial(lambda e, to_right, s, bufs: reduce_relay(s, e, bufs, to_right), s=s, bufs=bufs))

        def update(e, to_right, s=s, bufs=bufs):
            y = reduced(s, e, bufs, to_right)
            new = (xe[s][NL + e].astype(F32) - dmp[e] * y).astype(BF16)
            xe[s + 1][NL + e] = new
            halo_next(s + 1, e).start()
            halo_prev(s + 1, e).start()
            if s == SWEEPS - 1:
                gather_right(e, b).start()
                gather_left(e, b).start()
                smooth_ref[e] = new
                xa[e, b] = new

        pairs(update)

        def halo_in(e, carry, s=s):
            halo_next(s + 1, e).wait_recv()
            halo_prev(s + 1, e).wait_recv()
            return carry

        lax.fori_loop(0, NL, halo_in, 0)

    def forward(e, to_right):
        if to_right:
            gather_right(e, lt).wait_recv()
            gather_on(e, True, lt).start()
        else:
            gather_left(e, rt).wait_recv()
            gather_on(e, False, rt).start()

    pairs(forward)

    def couple(e, carry):
        own = me * NL + e
        own_agg = agg_s[own]
        own_grp = grp_s[own_agg]
        x_own = xe[SWEEPS][NL + e]
        xg2[pl.ds(0, RB), pl.ds(0, NC)] = x_own
        xg2[pl.ds(0, RB), pl.ds(NC, NC)] = x_own
        for k in range(NBR):
            near_agg = agg_s[nbr_s[e, k]]
            near_grp = grp_s[near_agg]
            x_near = xe[SWEEPS][nearby(e, k)].astype(F32)
            in_agg = jnp.where(near_agg == own_agg, 1.0, 0.0).astype(F32)
            in_grp = jnp.where(near_grp == own_grp, 1.0, 0.0).astype(F32)
            xg2[pl.ds((k + 1) * RB, RB), pl.ds(0, NC)] = (x_near * in_agg).astype(BF16)
            xg2[pl.ds((k + 1) * RB, RB), pl.ds(NC, NC)] = (x_near * in_grp).astype(BF16)
        zs[e] = jnp.dot(a_v[e], xg2[...], preferred_element_type=F32).astype(BF16)
        return carry

    lax.fori_loop(0, NL, couple, 0)

    gbufs = (gsum, g_opp, g_plain, g_relay, g_r1, g_rp, g_rr)

    def contract(e, to_right):
        if to_right:
            gather_left(e, rt).wait_recv()
        else:
            gather_right(e, lt).wait_recv()
        gather_on(e, to_right, op).wait_recv()
        both = lax.dot_general(
            xa[e].reshape(ROWS, NC), zs[e], (((0,), (0,)), ((), ())), preferred_element_type=F32
        )
        gsum[e] = both.reshape(BLK, HR, 2 * NC)
        reduce_send(SWEEPS, e, gbufs, to_right)

    pairs(contract)
    pairs(lambda e, to_right: reduce_relay(SWEEPS, e, gbufs, to_right))

    def settle(e, to_right):
        both = reduced(SWEEPS, e, gbufs, to_right).astype(BF16)
        gx[xc, core * NL + e] = both[:, :NC]
        c8h[core * NL + e] = both[:, NC:]

    pairs(settle)

    mate = at(xc, zc, 1 - core)
    here = pl.ds(core * NL, NL)
    there = pl.ds((1 - core) * NL, NL)

    def mate_copies(span):
        return (
            remote(gx.at[xc, span], gx.at[xc, span], d_ss.at[0], d_rs.at[0], mate),
            remote(c8h.at[span], c8h.at[span], d_ss.at[1], d_rs.at[1], mate),
        )

    for copy in mate_copies(here):
        copy.start()
    for copy in mate_copies(there):
        copy.wait_recv()

    def x_copies(dx, owner):
        to = lax.rem(xc + dx, NX)
        dev = at(to, zc, core)
        return (
            remote(gx.at[owner], gx.at[owner], x_ss.at[dx - 1, 0], x_rs.at[dx - 1, 0], dev),
            remote(hs.at[to], hx.at[owner], x_ss.at[dx - 1, 1], x_rs.at[dx - 1, 1], dev),
        )

    for dx in range(1, NX):
        x_copies(dx, xc)[0].start()
    for dx in range(NX):
        to = lax.rem(xc + dx, NX)
        acc = jnp.zeros((HR, NC), F32)
        for i in range(2 * NL):
            g = grp_s[agg_s[(me // 2) * (2 * NL) + i]]
            acc = acc + jnp.where(g == 2 * to + core, 1.0, 0.0).astype(F32) * c8h[i].astype(F32)
        if dx:
            hs[to] = acc.astype(BF16)
            x_copies(dx, xc)[1].start()
        else:
            hx[xc] = acc.astype(BF16)
    for dx in range(1, NX):
        for copy in x_copies(dx, lax.rem(xc + NX - dx, NX)):
            copy.wait_recv()

    zh, zl = zc // zl_n, lax.rem(zc, zl_n)

    def l1_copy(d, owner):
        dev = at(xc, zh * zl_n + lax.rem(zl + d, zl_n), core)
        return remote(l1.at[owner], l1.at[owner], l1_ss.at[d - 1], l1_rs.at[d - 1], dev)

    def l2_copy(d, owner):
        dev = at(xc, lax.rem(zh + d, zh_n) * zl_n + zl, core)
        return remote(l2.at[owner], l2.at[owner], l2_ss.at[d - 1], l2_rs.at[d - 1], dev)

    def summed(ref, n):
        acc = ref[0].astype(F32)
        for i in range(1, n):
            acc = acc + ref[i].astype(F32)
        return acc

    l1[zl] = summed(hx, NX).astype(BF16)
    for d in range(1, zl_n):
        l1_copy(d, zl).start()

    for h in range(HR // 16):
        part = gx[:, :, h * 16 : (h + 1) * 16, :].reshape(512, NC)
        sums = jnp.dot(km[...], part, preferred_element_type=F32)
        pb[:, h * 16 : (h + 1) * 16, :] = sums.reshape(2 * nz, 16, NC).astype(BF16)

    def z_copy(dz):
        to = lax.rem(zc + dz, nz)
        return remote(
            pb.at[pl.ds(to * 2, 2)], rz.at[dz], z_ss.at[dz - 1], z_rs.at[dz - 1], at(xc, to, core)
        )

    def z_start(dz, carry):
        z_copy(dz).start()
        return carry

    lax.fori_loop(1, nz, z_start, 0)

    for d in range(1, zl_n):
        l1_copy(d, lax.rem(zl + zl_n - d, zl_n)).wait_recv()
    l2[zh] = summed(l1, zl_n).astype(BF16)
    for d in range(1, zh_n):
        l2_copy(d, zh).start()
    for d in range(1, zh_n):
        l2_copy(d, lax.rem(zh + zh_n - d, zh_n)).wait_recv()
    mine = 2 * xc + core
    ll[mine] = summed(l2, zh_n)

    def final_copy(i, owner):
        return remote(ll.at[owner], ll.at[owner], f_ss.at[i], f_rs.at[i], line[i])

    for i in range(len(line)):
        final_copy(i, mine).start()

    def z_sum(dz, acc):
        z_copy(dz).wait_recv()
        return acc + rz[dz].astype(F32)

    coarse_ref[...] = lax.fori_loop(1, nz, z_sum, pb[pl.ds(zc * 2, 2)].astype(F32))

    i = 0
    for dx in range(NX):
        for dc in range(2):
            if dx or dc:
                owner = 2 * lax.rem(xc + NX - dx, NX) + lax.rem(core + dc, 2)
                final_copy(i, owner).wait_recv()
                i += 1
    last_ref[...] = ll[...]

    h0n.wait_send()
    h0p.wait_send()

    def halo_out(e, carry):
        for s in range(SWEEPS):
            halo_next(s + 1, e).wait_send()
            halo_prev(s + 1, e).wait_send()
        gather_right(e, b).wait_send()
        gather_left(e, b).wait_send()
        return carry

    lax.fori_loop(0, NL, halo_out, 0)
    pairs(lambda e, to_right: gather_on(e, to_right, lt if to_right else rt).wait_send())
    for s in range(SWEEPS):
        reduce_drain(
            s,
            (ysum, y_opp.at[s], y_plain.at[s], y_relay.at[s], y_r1.at[s], y_rp.at[s], y_rr.at[s]),
        )
    reduce_drain(SWEEPS, gbufs)
    for copy in mate_copies(here):
        copy.wait_send()
    for dx in range(1, NX):
        for copy in x_copies(dx, xc):
            copy.wait_send()
    for d in range(1, zl_n):
        l1_copy(d, zl).wait_send()
    for d in range(1, zh_n):
        l2_copy(d, zh).wait_send()
    for i in range(len(line)):
        final_copy(i, mine).wait_send()

    def z_out(dz, carry):
        z_copy(dz).wait_send()
        return carry

    lax.fori_loop(1, nz, z_out, 0)


def body(nz, diag, nbrs, neighbours, damping, bases, agglomerate, group):
    vmem = pl.BlockSpec(memory_space=pltpu.VMEM)
    smem = pl.BlockSpec(memory_space=pltpu.SMEM)
    hbm = pl.BlockSpec(memory_space=pltpu.HBM)
    zl_n = min(4, nz)
    dma = pltpu.SemaphoreType.DMA
    V = pltpu.VMEM
    el = (NL, RB, NC)
    gel = (NL, HR, 2 * NC)
    scratch = [
        V((NL, ROWS, KK), BF16),
        *[V((3 * NL, RB, NC), BF16) for _ in range(SWEEPS + 1)],
        V((KK, NC), BF16),
        V((KK, 2 * NC), BF16),
        V((NL, RB, NC), F32),
        V((NL, BLK, RB, NC), F32),
        *[V((SWEEPS, *el), BF16) for _ in range(6)],
        V((NL, BLK, RB, NC), BF16),
        V((NL, ROWS, 2 * NC), BF16),
        V((NL, BLK, HR, 2 * NC), F32),
        *[V(gel, BF16) for _ in range(6)],
        V((NX, 2 * NL, HR, NC), BF16),
        V((2 * NL, HR, NC), BF16),
        V((NX, HR, NC), BF16),
        V((NX, HR, NC), BF16),
        V((2 * nz * 16, 512), BF16),
        V((2 * nz, HR, NC), BF16),
        V((nz, 2, HR, NC), BF16),
        V((zl_n, HR, NC), BF16),
        V((nz // zl_n, HR, NC), BF16),
        V((8, HR, NC), F32),
        dma((NL,)),
        dma,
        dma((SWEEPS + 1, 2, NL)),
        dma((SWEEPS + 1, 2, NL)),
        dma((SWEEPS + 1, 3, NL)),
        dma((SWEEPS + 1, 3, NL)),
        dma((3, NL)),
        dma((3, NL)),
        dma((2,)),
        dma((2,)),
        dma((NX - 1, 2)),
        dma((NX - 1, 2)),
        dma((nz - 1,)),
        dma((nz - 1,)),
        dma((3,)),
        dma((3,)),
        dma((3,)),
        dma((3,)),
        dma((2 * NX - 1,)),
        dma((2 * NX - 1,)),
    ]
    return pl.pallas_call(
        functools.partial(kernel, nz),
        out_shape=(
            jax.ShapeDtypeStruct((NL, RB, NC), BF16),
            jax.ShapeDtypeStruct((2, HR, NC), F32),
            jax.ShapeDtypeStruct((8, HR, NC), F32),
        ),
        in_specs=[smem, smem, smem, vmem, hbm, hbm, hbm],
        out_specs=(vmem, vmem, vmem),
        scratch_shapes=scratch,
        compiler_params=pltpu.CompilerParams(
            collective_id=0, has_side_effects=True, vmem_limit_bytes=48 * 1024 * 1024
        ),
        name="galerkin",
    )(neighbours, agglomerate, group, damping, diag, nbrs, bases)


def solution(mesh):
    nz = mesh.shape["elem"] // (2 * NX)
    return jax.shard_map(
        functools.partial(body, nz),
        mesh=mesh,
        in_specs=(
            P("elem", None, "blk"),
            P("elem", None, None, "blk"),
            P("elem", None),
            P("elem", "blk"),
            P("elem", "blk", None),
            P(),
            P(),
        ),
        out_specs=(P("elem", "blk", None), P("elem", "blk", None), P(None, "blk", None)),
        check_vma=False,
    )
```

```python
import functools

import jax
import jax.numpy as jnp
from jax import lax
from jax.experimental import pallas as pl
from jax.experimental.pallas import tpu as pltpu
from jax.sharding import PartitionSpec as P

MESH = pl.DeviceIdType.MESH
F32 = jnp.float32
BF16 = jnp.bfloat16
NL = 4
NBR = 6
BLK = 4
NX = 4
NC = 128
RB = 128
ROWS = RB * BLK
KK = (NBR + 1) * RB
HR = NC // BLK
SWEEPS = 2
LIMIT = 62 * 1024 * 1024


def remote(src, dst, send_sem, recv_sem, device):
    return pltpu.make_async_remote_copy(
        src_ref=src,
        dst_ref=dst,
        send_sem=send_sem,
        recv_sem=recv_sem,
        device_id=device,
        device_id_type=MESH,
    )


def kernel(
    nz,
    nbr_h,
    agg_h,
    grp_h,
    damp_h,
    diag_hbm,
    nbrs_hbm,
    bases_hbm,
    smooth_ref,
    coarse_ref,
    last_ref,
    nbr_s,
    agg_s,
    grp_s,
    damp_v,
    a_v,
    xe0,
    xe1,
    xe2,
    xg,
    xg2,
    dmp,
    ysum,
    y_out0,
    y_out1,
    y_in0,
    y_in1,
    xt,
    xa,
    zs,
    h_out,
    h_in,
    g_out,
    g_in,
    gx,
    c8h,
    hs,
    hx,
    km,
    pb,
    rz,
    rfar,
    four,
    l1,
    l2,
    ll,
    s_sem,
    a_sem,
    up_sem,
    down_sem,
    halo0_ss,
    halo0_rs,
    halo_ss,
    halo_rs,
    y_ss,
    y_rs,
    ag_ss,
    ag_rs,
    gh_ss,
    gh_rs,
    d_ss,
    d_rs,
    x_ss,
    x_rs,
    z_ss,
    z_rs,
    l1_ss,
    l1_rs,
    l2_ss,
    l2_rs,
    f_ss,
    f_rs,
):
    xe = (xe0, xe1, xe2)
    y_out = (y_out0, y_out1)
    y_in = (y_in0, y_in1)
    ne = nz * NX * 2
    zl_n = min(4, nz)
    zh_n = nz // zl_n
    me = lax.axis_index("elem")
    b = lax.axis_index("blk")
    core = lax.rem(me, 2)
    zc = lax.rem(me // 2, nz)
    xc = me // (2 * nz)
    rt = lax.rem(b + 1, BLK)
    op = lax.rem(b + 2, BLK)
    lt = lax.rem(b + 3, BLK)
    nxt = (lax.rem(me + 1, ne), b)
    prv = (lax.rem(me + ne - 1, ne), b)
    right, left, across = (me, rt), (me, lt), (me, op)

    def at(x, z, c):
        return ((x * nz + z) * 2 + c, b)

    above = at(xc, lax.rem(zc + 1, nz), core)
    below = at(xc, lax.rem(zc + nz - 1, nz), core)
    line = []
    for dx in range(NX):
        for dc in range(2):
            if dx or dc:
                line.append(at(lax.rem(xc + dx, NX), zc, lax.rem(core + dc, 2)))

    drains = []

    def finish():
        for drain in drains:
            drain()
        drains.clear()

    own_in = pltpu.make_async_copy(bases_hbm, xe[0].at[pl.ds(NL, NL)], s_sem.at[0])
    own_in.start()

    barrier = pltpu.get_barrier_semaphore()
    partners = [across, nxt, prv, right, left, above, below, *line]
    for dev in partners:
        pl.semaphore_signal(barrier, inc=1, device_id=dev, device_id_type=MESH)
    small = [
        pltpu.make_async_copy(src, dst, s_sem.at[i + 1])
        for i, (src, dst) in enumerate(
            ((damp_h, damp_v), (nbr_h, nbr_s), (agg_h, agg_s), (grp_h, grp_s))
        )
    ]
    for copy in small:
        copy.start()
    own_in.wait()
    pl.semaphore_wait(barrier, len(partners))

    h0n = remote(xe[0].at[pl.ds(NL, NL)], xe[0].at[pl.ds(0, NL)], halo0_ss.at[0], halo0_rs.at[0], nxt)
    h0p = remote(
        xe[0].at[pl.ds(NL, NL)], xe[0].at[pl.ds(2 * NL, NL)], halo0_ss.at[1], halo0_rs.at[1], prv
    )
    h0n.start()
    h0p.start()
    drains.append(h0n.wait_send)
    drains.append(h0p.wait_send)

    def load_a(e, carry):
        pltpu.make_async_copy(
            diag_hbm.at[e], a_v.at[e, :, pl.ds(0, RB)], a_sem.at[e]
        ).start()
        for k in range(NBR):
            pltpu.make_async_copy(
                nbrs_hbm.at[e, k],
                a_v.at[e, :, pl.ds((k + 1) * RB, RB)],
                a_sem.at[e],
            ).start()
        return carry

    lax.fori_loop(0, NL, load_a, 0)

    last_news = nz // 2 - 1
    news = [0]

    def pass_on():
        j = news[0]
        news[0] += 1
        if 1 <= j <= last_news:
            pl.semaphore_wait(up_sem, 1)
            pl.semaphore_wait(down_sem, 1)
        if j < last_news:
            pl.semaphore_signal(up_sem, inc=1, device_id=above, device_id_type=MESH)
            pl.semaphore_signal(down_sem, inc=1, device_id=below, device_id_type=MESH)

    for copy in small:
        copy.wait()
    for e in range(NL):
        dmp[e] = jnp.broadcast_to(damp_v[pl.ds(e, 1), :], (RB, NC)).T

    lane = lax.broadcasted_iota(jnp.int32, (16, 512), 1)
    row = lax.broadcasted_iota(jnp.int32, (16, 512), 0)

    def place(i, slots):
        xx, cc, j = i // 8, lax.rem(i // 4, 2), lax.rem(i, 4)
        a = agg_s[((xx * nz + zc) * 2 + cc) * NL + j]
        dev = a // 2
        mine = (lax.rem(dev, 2) == core) & (dev // (2 * nz) == xc)
        slot = jnp.where(mine, lax.rem(dev // 2, nz) * 2 + lax.rem(a, 2), -1)
        return jnp.where(lane // 16 == i, slot, slots)

    slots = lax.fori_loop(0, 32, place, jnp.full((16, 512), -1, jnp.int32))
    same_row = row == lax.rem(lane, 16)

    def fill(s, carry):
        km[pl.ds(pl.multiple_of(s * 16, 16), 16), :] = jnp.where(
            (slots == s) & same_row, 1.0, 0.0
        ).astype(BF16)
        return carry

    lax.fori_loop(0, 2 * nz, fill, 0)

    h0n.wait_recv()
    h0p.wait_recv()
    pass_on()

    first = (me - 1) * NL

    def nearby(e, k):
        return jnp.clip(nbr_s[e, k] - first, 0, 3 * NL - 1)

    def wait_a(e):
        pltpu.make_async_copy(a_v.at[e], a_v.at[e], a_sem.at[e]).wait()

    def y_copy(s, kind, e, dev):
        return remote(y_out[s].at[kind, e], y_in[s].at[kind, e], y_ss.at[s, kind, e], y_rs.at[s, kind, e], dev)

    def halo_next(st, e):
        return remote(
            xe[st].at[NL + e], xe[st].at[e], halo_ss.at[st - 1, 0, e], halo_rs.at[st - 1, 0, e], nxt
        )

    def halo_prev(st, e):
        return remote(
            xe[st].at[NL + e],
            xe[st].at[2 * NL + e],
            halo_ss.at[st - 1, 1, e],
            halo_rs.at[st - 1, 1, e],
            prv,
        )

    def sides(to_right):
        return (right, rt, left, lt) if to_right else (left, lt, right, rt)

    def pairs(step):
        def one(i, carry):
            step(i, True)
            step(i + 2, False)
            return carry

        lax.fori_loop(0, 2, one, 0)

    def gather_right(e, owner):
        return remote(
            xt.at[e], xa.at[e, owner], ag_ss.at[0, e], ag_rs.at[0, e], right
        )

    def gather_left(e, owner):
        return remote(
            xt.at[e], xa.at[e, owner], ag_ss.at[1, e], ag_rs.at[1, e], left
        )

    def gather_on(e, to_right, owner):
        near = sides(to_right)[0]
        return remote(xa.at[e, owner], xa.at[e, owner], ag_ss.at[2, e], ag_rs.at[2, e], near)

    def near_of(i):
        return lax.rem(b + 1 + 2 * i, BLK)

    for s in range(SWEEPS):

        def product(e, s=s):
            if s == 0:
                wait_a(e)
            xg[pl.ds(0, RB), :] = xe[s][NL + e]
            for k in range(NBR):
                xg[pl.ds((k + 1) * RB, RB), :] = xe[s][nearby(e, k)]
            y = jnp.dot(a_v[e], xg[...], preferred_element_type=F32)
            ysum[e] = y.reshape(BLK, RB, NC)

        def send_relayed(i, carry, s=s):
            product(i)
            near, far = near_of(i), near_of(i + 1)
            y_out[s][2, i] = ysum[i, op].astype(BF16)
            y_copy(s, 2, i, (me, near)).start()
            y_out[s][1 - i, i] = ysum[i, far].astype(BF16)
            y_copy(s, 1 - i, i, (me, far)).start()
            return carry

        def send_direct(e, carry, s=s):
            product(e)
            for kind, to in ((2, op), (0, rt), (1, lt)):
                y_out[s][kind, e] = ysum[e, to].astype(BF16)
                y_copy(s, kind, e, (me, to)).start()
            return carry

        def relay(i, carry, s=s):
            near = near_of(i)
            y_copy(s, 2, i, (me, near)).wait_recv()
            y_out[s][i, i] = (ysum[i, near] + y_in[s][2, i].astype(F32)).astype(BF16)
            y_copy(s, i, i, (me, near)).start()
            return carry

        lax.fori_loop(0, 2, send_relayed, 0)
        lax.fori_loop(2, NL, send_direct, 0)
        pass_on()
        lax.fori_loop(0, 2, relay, 0)

        def y_sent(e, carry, s=s):
            for kind in range(3):
                y_copy(s, kind, e, right).wait_send()
            return carry

        drains.append(functools.partial(lax.fori_loop, 0, NL, y_sent, 0))

        def update(e, direct, s=s):
            for kind in (0, 1, 2)[: 3 if direct else 2]:
                y_copy(s, kind, e, right).wait_recv()
            y = ysum[e, b] + y_in[s][0, e].astype(F32) + y_in[s][1, e].astype(F32)
            if direct:
                y = y + y_in[s][2, e].astype(F32)
            new = (xe[s][NL + e].astype(F32) - dmp[e] * y).astype(BF16)
            xe[s + 1][NL + e] = new
            halo_next(s + 1, e).start()
            halo_prev(s + 1, e).start()
            if s == SWEEPS - 1:
                turned = new.astype(F32).T.astype(BF16)
                xt[e] = turned
                gather_right(e, b).start()
                gather_left(e, b).start()
                smooth_ref[e] = new
                xa[e, b] = turned

        def update_relayed(e, carry, update=update):
            update(e, False)
            return carry

        def update_direct(e, carry, update=update):
            update(e, True)
            return carry

        lax.fori_loop(2, NL, update_direct, 0)
        lax.fori_loop(0, 2, update_relayed, 0)
        pass_on()

        def halo_in(e, carry, s=s):
            halo_next(s + 1, e).wait_recv()
            halo_prev(s + 1, e).wait_recv()
            return carry

        lax.fori_loop(0, NL, halo_in, 0)

        def halo_out(e, carry, s=s):
            halo_next(s + 1, e).wait_send()
            halo_prev(s + 1, e).wait_send()
            if s == SWEEPS - 1:
                gather_right(e, b).wait_send()
                gather_left(e, b).wait_send()
            return carry

        drains.append(functools.partial(lax.fori_loop, 0, NL, halo_out, 0))
        pass_on()
    def forward(e, to_right):
        if to_right:
            gather_right(e, lt).wait_recv()
            gather_on(e, True, lt).start()
        else:
            gather_left(e, rt).wait_recv()
            gather_on(e, False, rt).start()

    pairs(forward)
    drains.append(
        lambda: pairs(lambda e, to_right: gather_on(e, to_right, lt if to_right else rt).wait_send())
    )

    def couple(e, carry):
        own = me * NL + e
        own_agg = agg_s[own]
        own_grp = grp_s[own_agg]
        x_own = xe[SWEEPS][NL + e]
        xg2[pl.ds(0, RB), pl.ds(0, NC)] = x_own
        xg2[pl.ds(0, RB), pl.ds(NC, NC)] = x_own
        for k in range(NBR):
            near_agg = agg_s[nbr_s[e, k]]
            near_grp = grp_s[near_agg]
            x_near = xe[SWEEPS][nearby(e, k)].astype(F32)
            in_agg = jnp.where(near_agg == own_agg, 1.0, 0.0).astype(F32)
            in_grp = jnp.where(near_grp == own_grp, 1.0, 0.0).astype(F32)
            xg2[pl.ds((k + 1) * RB, RB), pl.ds(0, NC)] = (x_near * in_agg).astype(BF16)
            xg2[pl.ds((k + 1) * RB, RB), pl.ds(NC, NC)] = (x_near * in_grp).astype(BF16)
        zs[e] = jnp.dot(a_v[e], xg2[...], preferred_element_type=F32).astype(BF16)
        return carry

    lax.fori_loop(0, NL, couple, 0)
    pass_on()

    def contract(e, to_right):
        if to_right:
            gather_left(e, rt).wait_recv()
        else:
            gather_right(e, lt).wait_recv()
        gather_on(e, to_right, op).wait_recv()
        rows = jnp.concatenate([xa[e, r] for r in range(BLK)], axis=1)
        both = jnp.dot(rows, zs[e], preferred_element_type=F32)
        both = both.astype(BF16).reshape(BLK, HR, 2 * NC)
        g_out[:, e] = both[:, :, :NC]
        h_out[:, e] = both[:, :, NC:]

    pairs(contract)

    def gh_copy(which, kind, to):
        out, into = ((h_out, h_in), (g_out, g_in))[which]
        return remote(
            out.at[to], into.at[kind], gh_ss.at[which, kind], gh_rs.at[which, kind], (me, to)
        )

    for which in range(2):
        for kind, to in ((2, op), (0, rt), (1, lt)):
            gh_copy(which, kind, to).start()
            drains.append(gh_copy(which, kind, to).wait_send)

    def gh_sum(which):
        out, into = ((h_out, h_in), (g_out, g_in))[which]
        acc = out[b].astype(F32)
        for kind in range(3):
            gh_copy(which, kind, rt).wait_recv()
            acc = acc + into[kind].astype(F32)
        return acc.astype(BF16)

    mate = at(xc, zc, 1 - core)
    here = pl.ds(core * NL, NL)
    there = pl.ds((1 - core) * NL, NL)

    def mate_h(span):
        return remote(c8h.at[span], c8h.at[span], d_ss.at[0], d_rs.at[0], mate)

    def mate_g(span):
        return remote(gx.at[xc, span], gx.at[xc, span], d_ss.at[1], d_rs.at[1], mate)

    c8h[here] = gh_sum(0)
    mate_h(here).start()
    drains.append(mate_h(here).wait_send)
    gx[xc, here] = gh_sum(1)
    mate_g(here).start()
    drains.append(mate_g(here).wait_send)
    def x_g(dx, owner):
        dev = at(lax.rem(xc + dx, NX), zc, core)
        return remote(gx.at[owner], gx.at[owner], x_ss.at[dx - 1, 0], x_rs.at[dx - 1, 0], dev)

    def x_h(dx, owner):
        to = lax.rem(xc + dx, NX)
        return remote(
            hs.at[to], hx.at[owner], x_ss.at[dx - 1, 1], x_rs.at[dx - 1, 1], at(to, zc, core)
        )

    groups = [grp_s[agg_s[(me // 2) * (2 * NL) + i]] for i in range(2 * NL)]
    mate_h(there).wait_recv()
    for dx in (2, 1, 3, 0):
        to = lax.rem(xc + dx, NX)
        acc = jnp.zeros((HR, NC), F32)
        for i in range(2 * NL):
            acc = acc + jnp.where(groups[i] == 2 * to + core, 1.0, 0.0).astype(F32) * c8h[i].astype(
                F32
            )
        if dx:
            hs[to] = acc.astype(BF16)
            x_h(dx, xc).start()
            drains.append(x_h(dx, xc).wait_send)
        else:
            hx[xc] = acc.astype(BF16)
    mate_g(there).wait_recv()
    for dx in (2, 1, 3):
        x_g(dx, xc).start()
        drains.append(x_g(dx, xc).wait_send)

    zh, zl = zc // zl_n, lax.rem(zc, zl_n)

    def l1_copy(d, owner):
        dev = at(xc, zh * zl_n + lax.rem(zl + d, zl_n), core)
        return remote(l1.at[owner], l1.at[owner], l1_ss.at[d - 1], l1_rs.at[d - 1], dev)

    def l2_copy(d, owner):
        dev = at(xc, lax.rem(zh + d, zh_n) * zl_n + zl, core)
        return remote(l2.at[owner], l2.at[owner], l2_ss.at[d - 1], l2_rs.at[d - 1], dev)

    def summed(ref, n):
        acc = ref[0].astype(F32)
        for i in range(1, n):
            acc = acc + ref[i].astype(F32)
        return acc

    for dx in range(1, NX):
        x_h(dx, lax.rem(xc + NX - dx, NX)).wait_recv()
    l1[zl] = summed(hx, NX).astype(BF16)
    for d in range(1, zl_n):
        l1_copy(d, zl).start()
        drains.append(l1_copy(d, zl).wait_send)

    for dx in range(1, NX):
        x_g(dx, lax.rem(xc + NX - dx, NX)).wait_recv()
    for h in range(HR // 16):
        part = gx[:, :, h * 16 : (h + 1) * 16, :].reshape(512, NC)
        sums = jnp.dot(km[...], part, preferred_element_type=F32)
        pb[:, h * 16 : (h + 1) * 16, :] = sums.reshape(2 * nz, 16, NC).astype(BF16)

    def chunk(d):
        return pb.at[pl.ds(lax.rem(zc + nz + d, nz) * 2, 2)]

    def place_z(d):
        return at(xc, lax.rem(zc + nz + d, nz), core)

    eight = (1 - 2 * core) * 4

    def z_far(side, k):
        i = side * 3 + k - 1
        d = (1 - 2 * side) * k
        return remote(
            chunk((1 - 2 * side) * (k + 4)), rfar.at[side, k - 1], z_ss.at[i], z_rs.at[i], place_z(d)
        )

    def z_eight():
        return remote(chunk(8), rz.at[6], z_ss.at[6], z_rs.at[6], place_z(eight))

    def z_near(side, k):
        i = side * 3 + k - 1
        d = (1 - 2 * side) * k
        return remote(chunk(d), rz.at[i], z_ss.at[7 + i], z_rs.at[7 + i], place_z(d))

    def z_last(side):
        d = (1 - 2 * side) * 4
        return remote(four.at[side], rz.at[7 + side], z_ss.at[13 + side], z_rs.at[13 + side], place_z(d))

    z_eight().start()
    drains.append(z_eight().wait_send)
    for k in (3, 2, 1):
        for side in range(2):
            z_far(side, k).start()
            drains.append(z_far(side, k).wait_send)
    for k in (3, 2, 1):
        for side in range(2):
            z_near(side, k).start()
            drains.append(z_near(side, k).wait_send)

    for d in range(1, zl_n):
        l1_copy(d, lax.rem(zl + zl_n - d, zl_n)).wait_recv()
    l2[zh] = summed(l1, zl_n).astype(BF16)
    for d in range(1, zh_n):
        l2_copy(d, zh).start()
    sums = [chunk(4 - 8 * side)[...].astype(F32) for side in range(2)]
    for side in range(2):
        for k in (1, 2, 3):
            z_far(side, k).wait_recv()
            sums[side] = sums[side] + rfar[side, k - 1].astype(F32)
    z_eight().wait_recv()
    passed = rz[6].astype(F32)
    for side in range(2):
        share = jnp.where(core == side, 1.0, 0.0).astype(F32)
        four[side] = (sums[side] + share * passed).astype(BF16)
        z_last(side).start()
    finish()
    for d in range(1, zh_n):
        l2_copy(d, lax.rem(zh + zh_n - d, zh_n)).wait_recv()
    mine = 2 * xc + core
    ll[mine] = summed(l2, zh_n)

    def final_copy(i, owner):
        return remote(ll.at[owner], ll.at[owner], f_ss.at[i], f_rs.at[i], line[i])

    for i in range(len(line)):
        final_copy(i, mine).start()

    total = pb[pl.ds(zc * 2, 2)].astype(F32)
    for side in range(2):
        for k in (1, 2, 3):
            z_near(side, k).wait_recv()
            total = total + rz[side * 3 + k - 1].astype(F32)
    for side in range(2):
        z_last(side).wait_recv()
        total = total + rz[7 + side].astype(F32)
    coarse_ref[...] = total
    for side in range(2):
        z_last(side).wait_send()
    for d in range(1, zh_n):
        l2_copy(d, zh).wait_send()

    i = 0
    for dx in range(NX):
        for dc in range(2):
            if dx or dc:
                owner = 2 * lax.rem(xc + NX - dx, NX) + lax.rem(core + dc, 2)
                final_copy(i, owner).wait_recv()
                i += 1
    last_ref[...] = ll[...]
    for i in range(len(line)):
        final_copy(i, mine).wait_send()


def write_out(a, b, c, a_out, b_out, c_out, a_v, b_v, c_v, in_sem, out_sem):
    held = ((a, a_v, a_out), (b, b_v, b_out), (c, c_v, c_out))
    reads = [pltpu.make_async_copy(x, v, in_sem.at[i]) for i, (x, v, _) in enumerate(held)]
    writes = [pltpu.make_async_copy(v, o, out_sem.at[i]) for i, (_, v, o) in enumerate(held)]
    for read in reads:
        read.start()
    for read, write in zip(reads, writes):
        read.wait()
        write.start()
    for write in writes:
        write.wait()


def body(nz, diag, nbrs, neighbours, damping, bases, agglomerate, group):
    vmem = pl.BlockSpec(memory_space=pltpu.VMEM)
    hbm = pl.BlockSpec(memory_space=pltpu.HBM)
    zl_n = min(4, nz)
    dma = pltpu.SemaphoreType.DMA
    regular = pltpu.SemaphoreType.REGULAR
    V = pltpu.VMEM
    scratch = [
        pltpu.SMEM((NL, NBR), jnp.int32),
        pltpu.SMEM(agglomerate.shape, jnp.int32),
        pltpu.SMEM(group.shape, jnp.int32),
        V((NL, RB), F32),
        V((NL, ROWS, KK), BF16),
        *[V((3 * NL, RB, NC), BF16) for _ in range(SWEEPS + 1)],
        V((KK, NC), BF16),
        V((KK, 2 * NC), BF16),
        V((NL, RB, NC), F32),
        V((NL, BLK, RB, NC), F32),
        *[V((3, NL, RB, NC), BF16) for _ in range(4)],
        V((NL, RB, NC), BF16),
        V((NL, BLK, RB, NC), BF16),
        V((NL, ROWS, 2 * NC), BF16),
        V((BLK, NL, HR, NC), BF16),
        V((3, NL, HR, NC), BF16),
        V((BLK, NL, HR, NC), BF16),
        V((3, NL, HR, NC), BF16),
        V((NX, 2 * NL, HR, NC), BF16),
        V((2 * NL, HR, NC), BF16),
        V((NX, HR, NC), BF16),
        V((NX, HR, NC), BF16),
        V((2 * nz * 16, 512), BF16),
        V((2 * nz, HR, NC), BF16),
        V((9, 2, HR, NC), BF16),
        V((2, 3, 2, HR, NC), BF16),
        V((2, 2, HR, NC), BF16),
        V((zl_n, HR, NC), BF16),
        V((nz // zl_n, HR, NC), BF16),
        V((8, HR, NC), F32),
        dma((5,)),
        dma((NL,)),
        regular,
        regular,
        dma((2,)),
        dma((2,)),
        dma((SWEEPS, 2, NL)),
        dma((SWEEPS, 2, NL)),
        dma((SWEEPS, 3, NL)),
        dma((SWEEPS, 3, NL)),
        dma((3, NL)),
        dma((3, NL)),
        dma((2, 3)),
        dma((2, 3)),
        dma((2,)),
        dma((2,)),
        dma((NX - 1, 2)),
        dma((NX - 1, 2)),
        dma((nz - 1,)),
        dma((nz - 1,)),
        dma((3,)),
        dma((3,)),
        dma((3,)),
        dma((3,)),
        dma((2 * NX - 1,)),
        dma((2 * NX - 1,)),
    ]
    out = pl.pallas_call(
        functools.partial(kernel, nz),
        out_shape=(
            jax.ShapeDtypeStruct((NL, RB, NC), BF16),
            jax.ShapeDtypeStruct((2, HR, NC), F32),
            jax.ShapeDtypeStruct((8, HR, NC), F32),
        ),
        in_specs=[hbm] * 7,
        out_specs=(vmem, vmem, vmem),
        scratch_shapes=scratch,
        compiler_params=pltpu.CompilerParams(
            collective_id=0, has_side_effects=True, vmem_limit_bytes=LIMIT
        ),
        name="galerkin",
    )(neighbours, agglomerate, group, damping, diag, nbrs, bases)
    return pl.pallas_call(
        write_out,
        out_shape=tuple(jax.ShapeDtypeStruct(o.shape, o.dtype) for o in out),
        in_specs=[hbm] * 3,
        out_specs=(hbm,) * 3,
        scratch_shapes=[*[V(o.shape, o.dtype) for o in out], dma((3,)), dma((3,))],
        compiler_params=pltpu.CompilerParams(vmem_limit_bytes=LIMIT),
        name="write_out",
    )(*out)


def solution(mesh):
    nz = mesh.shape["elem"] // (2 * NX)
    return jax.shard_map(
        functools.partial(body, nz),
        mesh=mesh,
        in_specs=(
            P("elem", None, "blk"),
            P("elem", None, None, "blk"),
            P("elem", None),
            P("elem", "blk"),
            P("elem", "blk", None),
            P(),
            P(),
        ),
        out_specs=(P("elem", "blk", None), P("elem", "blk", None), P(None, "blk", None)),
        check_vma=False,
    )
```

```python
import functools

import jax
import jax.numpy as jnp
from jax import lax
from jax.experimental import pallas as pl
from jax.experimental.pallas import tpu as pltpu
from jax.sharding import PartitionSpec as P

MESH = pl.DeviceIdType.MESH
F32 = jnp.float32
BF16 = jnp.bfloat16
NL = 4
NBR = 6
BLK = 4
NX = 4
NC = 128
RB = 128
ROWS = RB * BLK
KK = (NBR + 1) * RB
HR = NC // BLK
SWEEPS = 2
LIMIT = 62 * 1024 * 1024


def remote(src, dst, send_sem, recv_sem, device):
    return pltpu.make_async_remote_copy(
        src_ref=src,
        dst_ref=dst,
        send_sem=send_sem,
        recv_sem=recv_sem,
        device_id=device,
        device_id_type=MESH,
    )


def kernel(
    nz,
    nbr_h,
    agg_h,
    grp_h,
    damp_h,
    diag_hbm,
    nbrs_hbm,
    bases_hbm,
    smooth_ref,
    coarse_ref,
    last_ref,
    nbr_s,
    agg_s,
    grp_s,
    damp_v,
    a_v,
    xe0,
    xe1,
    xe2,
    xg,
    xg2,
    dmp,
    ysum,
    y_out0,
    y_out1,
    y_in0,
    y_in1,
    xt,
    xa,
    zs,
    h_part,
    h_out,
    g_out,
    g_in,
    gx,
    hx,
    km,
    pb,
    rz,
    rfar,
    four,
    l1,
    l2,
    ll,
    s_sem,
    a_sem,
    up_sem,
    down_sem,
    side_sem,
    halo0_ss,
    halo0_rs,
    halo_ss,
    halo_rs,
    y_ss,
    y_rs,
    ag_ss,
    ag_rs,
    h_ss,
    h_rs,
    g_ss,
    g_rs,
    x_ss,
    x_rs,
    z_ss,
    z_rs,
    l1_ss,
    l1_rs,
    l2_ss,
    l2_rs,
    f_ss,
    f_rs,
):
    xe = (xe0, xe1, xe2)
    y_out = (y_out0, y_out1)
    y_in = (y_in0, y_in1)
    ne = nz * NX * 2
    zl_n = min(4, nz)
    zh_n = nz // zl_n
    me = lax.axis_index("elem")
    b = lax.axis_index("blk")
    core = lax.rem(me, 2)
    zc = lax.rem(me // 2, nz)
    xc = me // (2 * nz)
    rt = lax.rem(b + 1, BLK)
    op = lax.rem(b + 2, BLK)
    lt = lax.rem(b + 3, BLK)
    nxt = (lax.rem(me + 1, ne), b)
    prv = (lax.rem(me + ne - 1, ne), b)
    right, left, across = (me, rt), (me, lt), (me, op)

    def at(x, z, c):
        return ((x * nz + z) * 2 + c, b)

    above = at(xc, lax.rem(zc + 1, nz), core)
    below = at(xc, lax.rem(zc + nz - 1, nz), core)
    line = []
    for dx in range(NX):
        for dc in range(2):
            if dx or dc:
                line.append(at(lax.rem(xc + dx, NX), zc, lax.rem(core + dc, 2)))

    drains = []

    def finish():
        for drain in drains:
            drain()
        drains.clear()

    own_in = pltpu.make_async_copy(bases_hbm, xe[0].at[pl.ds(NL, NL)], s_sem.at[0])
    own_in.start()

    barrier = pltpu.get_barrier_semaphore()
    partners = [across, nxt, prv, right, left, above, below, *line]
    for dev in partners:
        pl.semaphore_signal(barrier, inc=1, device_id=dev, device_id_type=MESH)
    small = [
        pltpu.make_async_copy(src, dst, s_sem.at[i + 1])
        for i, (src, dst) in enumerate(
            ((damp_h, damp_v), (nbr_h, nbr_s), (agg_h, agg_s), (grp_h, grp_s))
        )
    ]
    for copy in small:
        copy.start()
    own_in.wait()
    pl.semaphore_wait(barrier, len(partners))

    h0n = remote(xe[0].at[pl.ds(NL, NL)], xe[0].at[pl.ds(0, NL)], halo0_ss.at[0], halo0_rs.at[0], nxt)
    h0p = remote(
        xe[0].at[pl.ds(NL, NL)], xe[0].at[pl.ds(2 * NL, NL)], halo0_ss.at[1], halo0_rs.at[1], prv
    )
    h0n.start()
    h0p.start()
    for dev in (right, left, across):
        pl.semaphore_signal(side_sem, inc=1, device_id=dev, device_id_type=MESH)
    drains.append(h0n.wait_send)
    drains.append(h0p.wait_send)

    def load_a(e, carry):
        pltpu.make_async_copy(
            diag_hbm.at[e], a_v.at[e, :, pl.ds(0, RB)], a_sem.at[e]
        ).start()
        for k in range(NBR):
            pltpu.make_async_copy(
                nbrs_hbm.at[e, k],
                a_v.at[e, :, pl.ds((k + 1) * RB, RB)],
                a_sem.at[e],
            ).start()
        return carry

    lax.fori_loop(0, NL, load_a, 0)

    last_news = nz // 2 - 1
    news = [0]

    def pass_on():
        j = news[0]
        news[0] += 1
        if 1 <= j <= last_news:
            pl.semaphore_wait(up_sem, 1)
            pl.semaphore_wait(down_sem, 1)
        if j < last_news:
            pl.semaphore_signal(up_sem, inc=1, device_id=above, device_id_type=MESH)
            pl.semaphore_signal(down_sem, inc=1, device_id=below, device_id_type=MESH)

    for copy in small:
        copy.wait()
    for e in range(NL):
        dmp[e] = jnp.broadcast_to(damp_v[pl.ds(e, 1), :], (RB, NC)).T

    lane = lax.broadcasted_iota(jnp.int32, (16, 512), 1)
    row = lax.broadcasted_iota(jnp.int32, (16, 512), 0)

    def place(i, slots):
        xx, cc, j = i // 8, lax.rem(i // 4, 2), lax.rem(i, 4)
        a = agg_s[((xx * nz + zc) * 2 + cc) * NL + j]
        dev = a // 2
        mine = (lax.rem(dev, 2) == core) & (dev // (2 * nz) == xc)
        slot = jnp.where(mine, lax.rem(dev // 2, nz) * 2 + lax.rem(a, 2), -1)
        return jnp.where(lane // 16 == i, slot, slots)

    slots = lax.fori_loop(0, 32, place, jnp.full((16, 512), -1, jnp.int32))
    same_row = row == lax.rem(lane, 16)

    def fill(s, carry):
        km[pl.ds(pl.multiple_of(s * 16, 16), 16), :] = jnp.where(
            (slots == s) & same_row, 1.0, 0.0
        ).astype(BF16)
        return carry

    lax.fori_loop(0, 2 * nz, fill, 0)

    h0n.wait_recv()
    h0p.wait_recv()
    pass_on()

    first = (me - 1) * NL

    def nearby(e, k):
        return jnp.clip(nbr_s[e, k] - first, 0, 3 * NL - 1)

    def wait_a(e):
        pltpu.make_async_copy(a_v.at[e], a_v.at[e], a_sem.at[e]).wait()

    def y_copy(s, kind, e, dev):
        return remote(y_out[s].at[kind, e], y_in[s].at[kind, e], y_ss.at[s, kind, e], y_rs.at[s, kind, e], dev)

    def halo_next(st, e):
        return remote(
            xe[st].at[NL + e], xe[st].at[e], halo_ss.at[st - 1, 0, e], halo_rs.at[st - 1, 0, e], nxt
        )

    def halo_prev(st, e):
        return remote(
            xe[st].at[NL + e],
            xe[st].at[2 * NL + e],
            halo_ss.at[st - 1, 1, e],
            halo_rs.at[st - 1, 1, e],
            prv,
        )

    def sides(to_right):
        return (right, rt, left, lt) if to_right else (left, lt, right, rt)

    def pairs(step):
        def one(i, carry):
            step(i, True)
            step(i + 2, False)
            return carry

        lax.fori_loop(0, 2, one, 0)

    def gather_right(e, owner):
        return remote(
            xt.at[e], xa.at[e, owner], ag_ss.at[0, e], ag_rs.at[0, e], right
        )

    def gather_left(e, owner):
        return remote(
            xt.at[e], xa.at[e, owner], ag_ss.at[1, e], ag_rs.at[1, e], left
        )

    def gather_on(e, to_right, owner):
        near = sides(to_right)[0]
        return remote(xa.at[e, owner], xa.at[e, owner], ag_ss.at[2, e], ag_rs.at[2, e], near)

    def near_of(i):
        return lax.rem(b + 1 + 2 * i, BLK)

    for s in range(SWEEPS):

        def product(e, s=s):
            if s == 0:
                wait_a(e)
            xg[pl.ds(0, RB), :] = xe[s][NL + e]
            for k in range(NBR):
                xg[pl.ds((k + 1) * RB, RB), :] = xe[s][nearby(e, k)]
            y = jnp.dot(a_v[e], xg[...], preferred_element_type=F32)
            ysum[e] = y.reshape(BLK, RB, NC)

        def send_relayed(i, carry, s=s):
            product(i)
            near, far = near_of(i), near_of(i + 1)
            y_out[s][2, i] = ysum[i, op].astype(BF16)
            y_copy(s, 2, i, (me, near)).start()
            y_out[s][1 - i, i] = ysum[i, far].astype(BF16)
            y_copy(s, 1 - i, i, (me, far)).start()
            return carry

        def send_direct(e, carry, s=s):
            product(e)
            for kind, to in ((2, op), (0, rt), (1, lt)):
                y_out[s][kind, e] = ysum[e, to].astype(BF16)
                y_copy(s, kind, e, (me, to)).start()
            return carry

        def relay(i, carry, s=s):
            near = near_of(i)
            y_copy(s, 2, i, (me, near)).wait_recv()
            y_out[s][i, i] = (ysum[i, near] + y_in[s][2, i].astype(F32)).astype(BF16)
            y_copy(s, i, i, (me, near)).start()
            return carry

        lax.fori_loop(0, 2, send_relayed, 0)
        lax.fori_loop(2, NL, send_direct, 0)
        pass_on()
        lax.fori_loop(0, 2, relay, 0)

        def y_sent(e, carry, s=s):
            for kind in range(3):
                y_copy(s, kind, e, right).wait_send()
            return carry

        drains.append(functools.partial(lax.fori_loop, 0, NL, y_sent, 0))

        def update(e, direct, s=s):
            for kind in (0, 1, 2)[: 3 if direct else 2]:
                y_copy(s, kind, e, right).wait_recv()
            y = ysum[e, b] + y_in[s][0, e].astype(F32) + y_in[s][1, e].astype(F32)
            if direct:
                y = y + y_in[s][2, e].astype(F32)
            new = (xe[s][NL + e].astype(F32) - dmp[e] * y).astype(BF16)
            xe[s + 1][NL + e] = new
            halo_next(s + 1, e).start()
            halo_prev(s + 1, e).start()
            if s == SWEEPS - 1:
                turned = new.astype(F32).T.astype(BF16)
                xt[e] = turned
                gather_right(e, b).start()
                gather_left(e, b).start()
                smooth_ref[e] = new
                xa[e, b] = turned

        def update_relayed(e, carry, update=update):
            update(e, False)
            return carry

        def update_direct(e, carry, update=update):
            update(e, True)
            return carry

        lax.fori_loop(2, NL, update_direct, 0)
        lax.fori_loop(0, 2, update_relayed, 0)
        pass_on()

        def halo_in(e, carry, s=s):
            halo_next(s + 1, e).wait_recv()
            halo_prev(s + 1, e).wait_recv()
            return carry

        lax.fori_loop(0, NL, halo_in, 0)

        def halo_out(e, carry, s=s):
            halo_next(s + 1, e).wait_send()
            halo_prev(s + 1, e).wait_send()
            if s == SWEEPS - 1:
                gather_right(e, b).wait_send()
                gather_left(e, b).wait_send()
            return carry

        drains.append(functools.partial(lax.fori_loop, 0, NL, halo_out, 0))
        pass_on()
    def forward(e, to_right):
        if to_right:
            gather_right(e, lt).wait_recv()
            gather_on(e, True, lt).start()
        else:
            gather_left(e, rt).wait_recv()
            gather_on(e, False, rt).start()

    pairs(forward)
    drains.append(
        lambda: pairs(lambda e, to_right: gather_on(e, to_right, lt if to_right else rt).wait_send())
    )

    def couple(e, carry):
        own = me * NL + e
        own_agg = agg_s[own]
        own_grp = grp_s[own_agg]
        x_own = xe[SWEEPS][NL + e]
        xg2[pl.ds(0, RB), pl.ds(0, NC)] = x_own
        xg2[pl.ds(0, RB), pl.ds(NC, NC)] = x_own
        for k in range(NBR):
            near_agg = agg_s[nbr_s[e, k]]
            near_grp = grp_s[near_agg]
            x_near = xe[SWEEPS][nearby(e, k)].astype(F32)
            in_agg = jnp.where(near_agg == own_agg, 1.0, 0.0).astype(F32)
            in_grp = jnp.where(near_grp == own_grp, 1.0, 0.0).astype(F32)
            xg2[pl.ds((k + 1) * RB, RB), pl.ds(0, NC)] = (x_near * in_agg).astype(BF16)
            xg2[pl.ds((k + 1) * RB, RB), pl.ds(NC, NC)] = (x_near * in_grp).astype(BF16)
        zs[e] = jnp.dot(a_v[e], xg2[...], preferred_element_type=F32).astype(BF16)
        return carry

    lax.fori_loop(0, NL, couple, 0)
    pass_on()

    def contract(e, to_right):
        if to_right:
            gather_left(e, rt).wait_recv()
        else:
            gather_right(e, lt).wait_recv()
        gather_on(e, to_right, op).wait_recv()
        rows = jnp.concatenate([xa[e, r] for r in range(BLK)], axis=1)
        both = jnp.dot(rows, zs[e], preferred_element_type=F32)
        g_out[:, e] = both[:, :NC].astype(BF16).reshape(BLK, HR, NC)
        h_part[e] = both[:, NC:]

    pairs(contract)

    def g_copy(kind, to):
        return remote(g_out.at[to], g_in.at[kind], g_ss.at[kind], g_rs.at[kind], (me, to))

    for kind, to in ((2, op), (0, rt), (1, lt)):
        g_copy(kind, to).start()
        drains.append(g_copy(kind, to).wait_send)

    groups = [grp_s[agg_s[me * NL + e]] for e in range(NL)]

    def group_sum(g, carry):
        acc = jnp.zeros((NC, NC), F32)
        for e in range(NL):
            acc = acc + jnp.where(groups[e] == g, 1.0, 0.0).astype(F32) * h_part[e]
        h_out[g] = acc.astype(BF16).reshape(BLK, HR, NC)
        return carry

    lax.fori_loop(0, 2 * NX, group_sum, 0)
    pl.semaphore_wait(side_sem, 3)

    def h_copy(dx, dc, dy):
        x, c, y = lax.rem(xc + dx, NX), lax.rem(core + dc, 2), lax.rem(b + dy, BLK)
        i = (dx * 2 + dc) * BLK + dy - 1
        dev = ((x * nz + zc) * 2 + c, y)
        return remote(h_out.at[2 * x + c, y], hx.at[(2 * xc + core) * BLK + b], h_ss.at[i], h_rs.at[i], dev)

    def h_arrival(dx, dc, dy):
        x, c, y = lax.rem(xc + NX - dx, NX), lax.rem(core + dc, 2), lax.rem(b + BLK - dy, BLK)
        i = (dx * 2 + dc) * BLK + dy - 1
        return remote(h_out.at[0, 0], hx.at[(2 * x + c) * BLK + y], h_ss.at[i], h_rs.at[i], right)

    others = [
        (dx, dc, dy)
        for dx in (2, 1, 3, 0)
        for dy in (2, 1, 3, 0)
        for dc in (1, 0)
        if dx or dc or dy
    ]
    for o in others:
        h_copy(*o).start()
        drains.append(h_copy(*o).wait_send)
    hx[(2 * xc + core) * BLK + b] = h_out[2 * xc + core, b]

    acc = g_out[b].astype(F32)
    for kind in (0, 1, 2):
        g_copy(kind, rt).wait_recv()
        acc = acc + g_in[kind].astype(F32)
    gx[2 * xc + core] = acc.astype(BF16)

    def x_g(i, owner):
        return remote(gx.at[owner], gx.at[owner], x_ss.at[i], x_rs.at[i], line[i])

    def line_owner(i):
        k = i + 1
        return 2 * lax.rem(xc + NX - k // 2, NX) + lax.rem(core + k % 2, 2)

    for i in (3, 4, 1, 2, 5, 6, 0):
        x_g(i, 2 * xc + core).start()
        drains.append(x_g(i, 2 * xc + core).wait_send)
    zh, zl = zc // zl_n, lax.rem(zc, zl_n)

    def l1_copy(d, owner):
        dev = at(xc, zh * zl_n + lax.rem(zl + d, zl_n), core)
        return remote(l1.at[owner], l1.at[owner], l1_ss.at[d - 1], l1_rs.at[d - 1], dev)

    def l2_copy(d, owner):
        dev = at(xc, lax.rem(zh + d, zh_n) * zl_n + zl, core)
        return remote(l2.at[owner], l2.at[owner], l2_ss.at[d - 1], l2_rs.at[d - 1], dev)

    def summed(ref, n):
        acc = ref[0].astype(F32)
        for i in range(1, n):
            acc = acc + ref[i].astype(F32)
        return acc

    for o in others:
        h_arrival(*o).wait_recv()
    l1[zl] = summed(hx, 2 * NX * BLK).astype(BF16)
    for d in range(1, zl_n):
        l1_copy(d, zl).start()
        drains.append(l1_copy(d, zl).wait_send)

    for i in range(len(line)):
        x_g(i, line_owner(i)).wait_recv()
    for h in range(HR // 16):
        part = gx[:, :, h * 16 : (h + 1) * 16, :].reshape(512, NC)
        sums = jnp.dot(km[...], part, preferred_element_type=F32)
        pb[:, h * 16 : (h + 1) * 16, :] = sums.reshape(2 * nz, 16, NC).astype(BF16)

    def chunk(d):
        return pb.at[pl.ds(lax.rem(zc + nz + d, nz) * 2, 2)]

    def place_z(d):
        return at(xc, lax.rem(zc + nz + d, nz), core)

    eight = (1 - 2 * core) * 4

    def z_far(side, k):
        i = side * 3 + k - 1
        d = (1 - 2 * side) * k
        return remote(
            chunk((1 - 2 * side) * (k + 4)), rfar.at[side, k - 1], z_ss.at[i], z_rs.at[i], place_z(d)
        )

    def z_eight():
        return remote(chunk(8), rz.at[6], z_ss.at[6], z_rs.at[6], place_z(eight))

    def z_near(side, k):
        i = side * 3 + k - 1
        d = (1 - 2 * side) * k
        return remote(chunk(d), rz.at[i], z_ss.at[7 + i], z_rs.at[7 + i], place_z(d))

    def z_last(side):
        d = (1 - 2 * side) * 4
        return remote(four.at[side], rz.at[7 + side], z_ss.at[13 + side], z_rs.at[13 + side], place_z(d))

    for d in range(1, zl_n):
        l1_copy(d, lax.rem(zl + zl_n - d, zl_n)).wait_recv()
    l2[zh] = summed(l1, zl_n).astype(BF16)
    for d in range(1, zh_n):
        l2_copy(d, zh).start()

    z_eight().start()
    drains.append(z_eight().wait_send)
    for k in (3, 2, 1):
        for side in range(2):
            z_far(side, k).start()
            drains.append(z_far(side, k).wait_send)
    for k in (3, 2, 1):
        for side in range(2):
            z_near(side, k).start()
            drains.append(z_near(side, k).wait_send)

    finish()
    sums = [chunk(4 - 8 * side)[...].astype(F32) for side in range(2)]
    for side in range(2):
        for k in (1, 2, 3):
            z_far(side, k).wait_recv()
            sums[side] = sums[side] + rfar[side, k - 1].astype(F32)
    z_eight().wait_recv()
    passed = rz[6].astype(F32)
    for side in range(2):
        share = jnp.where(core == side, 1.0, 0.0).astype(F32)
        four[side] = (sums[side] + share * passed).astype(BF16)
        z_last(side).start()
    for d in range(1, zh_n):
        l2_copy(d, lax.rem(zh + zh_n - d, zh_n)).wait_recv()
    mine = 2 * xc + core
    ll[mine] = summed(l2, zh_n).astype(BF16)

    def final_copy(i, owner):
        return remote(ll.at[owner], ll.at[owner], f_ss.at[i], f_rs.at[i], line[i])

    for i in range(len(line)):
        final_copy(i, mine).start()

    total = pb[pl.ds(zc * 2, 2)].astype(F32)
    for side in range(2):
        for k in (1, 2, 3):
            z_near(side, k).wait_recv()
            total = total + rz[side * 3 + k - 1].astype(F32)
    for side in range(2):
        z_last(side).wait_recv()
        total = total + rz[7 + side].astype(F32)
    coarse_ref[...] = total
    for side in range(2):
        z_last(side).wait_send()
    for d in range(1, zh_n):
        l2_copy(d, zh).wait_send()

    for i in range(len(line)):
        final_copy(i, line_owner(i)).wait_recv()
    last_ref[...] = ll[...].astype(F32)
    for i in range(len(line)):
        final_copy(i, mine).wait_send()


def write_out(a, b, c, a_out, b_out, c_out, a_v, b_v, c_v, in_sem, out_sem):
    held = ((a, a_v, a_out), (b, b_v, b_out), (c, c_v, c_out))
    reads = [pltpu.make_async_copy(x, v, in_sem.at[i]) for i, (x, v, _) in enumerate(held)]
    writes = [pltpu.make_async_copy(v, o, out_sem.at[i]) for i, (_, v, o) in enumerate(held)]
    for read in reads:
        read.start()
    for read, write in zip(reads, writes):
        read.wait()
        write.start()
    for write in writes:
        write.wait()


def body(nz, diag, nbrs, neighbours, damping, bases, agglomerate, group):
    vmem = pl.BlockSpec(memory_space=pltpu.VMEM)
    hbm = pl.BlockSpec(memory_space=pltpu.HBM)
    zl_n = min(4, nz)
    dma = pltpu.SemaphoreType.DMA
    regular = pltpu.SemaphoreType.REGULAR
    V = pltpu.VMEM
    scratch = [
        pltpu.SMEM((NL, NBR), jnp.int32),
        pltpu.SMEM(agglomerate.shape, jnp.int32),
        pltpu.SMEM(group.shape, jnp.int32),
        V((NL, RB), F32),
        V((NL, ROWS, KK), BF16),
        *[V((3 * NL, RB, NC), BF16) for _ in range(SWEEPS + 1)],
        V((KK, NC), BF16),
        V((KK, 2 * NC), BF16),
        V((NL, RB, NC), F32),
        V((NL, BLK, RB, NC), F32),
        *[V((3, NL, RB, NC), BF16) for _ in range(4)],
        V((NL, RB, NC), BF16),
        V((NL, BLK, RB, NC), BF16),
        V((NL, ROWS, 2 * NC), BF16),
        V((NL, NC, NC), F32),
        V((2 * NX, BLK, HR, NC), BF16),
        V((BLK, NL, HR, NC), BF16),
        V((3, NL, HR, NC), BF16),
        V((2 * NX, NL, HR, NC), BF16),
        V((2 * NX * BLK, HR, NC), BF16),
        V((2 * nz * 16, 512), BF16),
        V((2 * nz, HR, NC), BF16),
        V((9, 2, HR, NC), BF16),
        V((2, 3, 2, HR, NC), BF16),
        V((2, 2, HR, NC), BF16),
        V((zl_n, HR, NC), BF16),
        V((nz // zl_n, HR, NC), BF16),
        V((8, HR, NC), BF16),
        dma((5,)),
        dma((NL,)),
        regular,
        regular,
        regular,
        dma((2,)),
        dma((2,)),
        dma((SWEEPS, 2, NL)),
        dma((SWEEPS, 2, NL)),
        dma((SWEEPS, 3, NL)),
        dma((SWEEPS, 3, NL)),
        dma((3, NL)),
        dma((3, NL)),
        dma((2 * NX * BLK - 1,)),
        dma((2 * NX * BLK - 1,)),
        dma((3,)),
        dma((3,)),
        dma((2 * NX - 1,)),
        dma((2 * NX - 1,)),
        dma((nz - 1,)),
        dma((nz - 1,)),
        dma((3,)),
        dma((3,)),
        dma((3,)),
        dma((3,)),
        dma((2 * NX - 1,)),
        dma((2 * NX - 1,)),
    ]
    out = pl.pallas_call(
        functools.partial(kernel, nz),
        out_shape=(
            jax.ShapeDtypeStruct((NL, RB, NC), BF16),
            jax.ShapeDtypeStruct((2, HR, NC), F32),
            jax.ShapeDtypeStruct((8, HR, NC), F32),
        ),
        in_specs=[hbm] * 7,
        out_specs=(vmem, vmem, vmem),
        scratch_shapes=scratch,
        compiler_params=pltpu.CompilerParams(
            collective_id=0, has_side_effects=True, vmem_limit_bytes=LIMIT
        ),
        name="galerkin",
    )(neighbours, agglomerate, group, damping, diag, nbrs, bases)
    return pl.pallas_call(
        write_out,
        out_shape=tuple(jax.ShapeDtypeStruct(o.shape, o.dtype) for o in out),
        in_specs=[hbm] * 3,
        out_specs=(hbm,) * 3,
        scratch_shapes=[*[V(o.shape, o.dtype) for o in out], dma((3,)), dma((3,))],
        compiler_params=pltpu.CompilerParams(vmem_limit_bytes=LIMIT),
        name="write_out",
    )(*out)


def solution(mesh):
    nz = mesh.shape["elem"] // (2 * NX)
    return jax.shard_map(
        functools.partial(body, nz),
        mesh=mesh,
        in_specs=(
            P("elem", None, "blk"),
            P("elem", None, None, "blk"),
            P("elem", None),
            P("elem", "blk"),
            P("elem", "blk", None),
            P(),
            P(),
        ),
        out_specs=(P("elem", "blk", None), P("elem", "blk", None), P(None, "blk", None)),
        check_vma=False,
    )
```

```python
import functools

import jax
import jax.numpy as jnp
from jax import lax
from jax.experimental import pallas as pl
from jax.experimental.pallas import tpu as pltpu
from jax.sharding import PartitionSpec as P

MESH = pl.DeviceIdType.MESH
F32 = jnp.float32
BF16 = jnp.bfloat16
NL = 4
NBR = 6
BLK = 4
NX = 4
NC = 128
RB = 128
ROWS = RB * BLK
KK = (NBR + 1) * RB
HR = NC // BLK
SWEEPS = 2
LIMIT = 62 * 1024 * 1024


def remote(src, dst, send_sem, recv_sem, device):
    return pltpu.make_async_remote_copy(
        src_ref=src,
        dst_ref=dst,
        send_sem=send_sem,
        recv_sem=recv_sem,
        device_id=device,
        device_id_type=MESH,
    )


def kernel(
    nz,
    nbr_h,
    agg_h,
    grp_h,
    damp_h,
    diag_hbm,
    nbrs_hbm,
    bases_hbm,
    smooth_ref,
    coarse_ref,
    last_ref,
    nbr_s,
    agg_s,
    grp_s,
    damp_v,
    a_v,
    xe0,
    xe1,
    xe2,
    xg,
    xg2,
    dmp,
    ysum,
    y_out0,
    y_out1,
    y_in0,
    y_in1,
    xt,
    xa,
    zs,
    h_part,
    h_out,
    g_out,
    g_in,
    gx,
    hx,
    km,
    pb,
    rz,
    rfar,
    four,
    l1,
    l2,
    ll,
    s_sem,
    a_sem,
    up_sem,
    down_sem,
    side_sem,
    halo0_ss,
    halo0_rs,
    halo_ss,
    halo_rs,
    y_ss,
    y_rs,
    ag_ss,
    ag_rs,
    h_ss,
    h_rs,
    g_ss,
    g_rs,
    x_ss,
    x_rs,
    z_ss,
    z_rs,
    l1_ss,
    l1_rs,
    l2_ss,
    l2_rs,
    f_ss,
    f_rs,
):
    xe = (xe0, xe1, xe2)
    y_out = (y_out0, y_out1)
    y_in = (y_in0, y_in1)
    ne = nz * NX * 2
    zl_n = min(4, nz)
    zh_n = nz // zl_n
    me = lax.axis_index("elem")
    b = lax.axis_index("blk")
    core = lax.rem(me, 2)
    zc = lax.rem(me // 2, nz)
    xc = me // (2 * nz)
    rt = lax.rem(b + 1, BLK)
    op = lax.rem(b + 2, BLK)
    lt = lax.rem(b + 3, BLK)
    nxt = (lax.rem(me + 1, ne), b)
    prv = (lax.rem(me + ne - 1, ne), b)
    right, left, across = (me, rt), (me, lt), (me, op)

    def at(x, z, c):
        return ((x * nz + z) * 2 + c, b)

    above = at(xc, lax.rem(zc + 1, nz), core)
    below = at(xc, lax.rem(zc + nz - 1, nz), core)
    line = []
    for dx in range(NX):
        for dc in range(2):
            if dx or dc:
                line.append(at(lax.rem(xc + dx, NX), zc, lax.rem(core + dc, 2)))

    drains = []

    def finish():
        for drain in drains:
            drain()
        drains.clear()

    own_in = pltpu.make_async_copy(bases_hbm, xe[0].at[pl.ds(NL, NL)], s_sem.at[0])
    own_in.start()

    barrier = pltpu.get_barrier_semaphore()
    partners = [across, nxt, prv, right, left, above, below, *line]
    for dev in partners:
        pl.semaphore_signal(barrier, inc=1, device_id=dev, device_id_type=MESH)
    small = [
        pltpu.make_async_copy(src, dst, s_sem.at[i + 1])
        for i, (src, dst) in enumerate(
            ((damp_h, damp_v), (nbr_h, nbr_s), (agg_h, agg_s), (grp_h, grp_s))
        )
    ]
    for copy in small:
        copy.start()
    own_in.wait()
    pl.semaphore_wait(barrier, len(partners))

    h0n = remote(xe[0].at[pl.ds(NL, NL)], xe[0].at[pl.ds(0, NL)], halo0_ss.at[0], halo0_rs.at[0], nxt)
    h0p = remote(
        xe[0].at[pl.ds(NL, NL)], xe[0].at[pl.ds(2 * NL, NL)], halo0_ss.at[1], halo0_rs.at[1], prv
    )
    h0n.start()
    h0p.start()
    for dev in (right, left, across):
        pl.semaphore_signal(side_sem, inc=1, device_id=dev, device_id_type=MESH)
    drains.append(h0n.wait_send)
    drains.append(h0p.wait_send)

    def load_a(e, carry):
        pltpu.make_async_copy(
            diag_hbm.at[e], a_v.at[e, :, pl.ds(0, RB)], a_sem.at[e]
        ).start()
        for k in range(NBR):
            pltpu.make_async_copy(
                nbrs_hbm.at[e, k],
                a_v.at[e, :, pl.ds((k + 1) * RB, RB)],
                a_sem.at[e],
            ).start()
        return carry

    lax.fori_loop(0, NL, load_a, 0)

    last_news = nz // 2 - 1
    news = [0]

    def pass_on():
        j = news[0]
        news[0] += 1
        if 1 <= j <= last_news:
            pl.semaphore_wait(up_sem, 1)
            pl.semaphore_wait(down_sem, 1)
        if j < last_news:
            pl.semaphore_signal(up_sem, inc=1, device_id=above, device_id_type=MESH)
            pl.semaphore_signal(down_sem, inc=1, device_id=below, device_id_type=MESH)

    for copy in small:
        copy.wait()
    for e in range(NL):
        dmp[e] = jnp.broadcast_to(damp_v[pl.ds(e, 1), :], (RB, NC)).T

    lane = lax.broadcasted_iota(jnp.int32, (16, 512), 1)
    row = lax.broadcasted_iota(jnp.int32, (16, 512), 0)

    def place(i, slots):
        xx, cc, j = i // 8, lax.rem(i // 4, 2), lax.rem(i, 4)
        a = agg_s[((xx * nz + zc) * 2 + cc) * NL + j]
        dev = a // 2
        mine = (lax.rem(dev, 2) == core) & (dev // (2 * nz) == xc)
        slot = jnp.where(mine, lax.rem(dev // 2, nz) * 2 + lax.rem(a, 2), -1)
        return jnp.where(lane // 16 == i, slot, slots)

    slots = lax.fori_loop(0, 32, place, jnp.full((16, 512), -1, jnp.int32))
    same_row = row == lax.rem(lane, 16)

    def fill(s, carry):
        km[pl.ds(pl.multiple_of(s * 16, 16), 16), :] = jnp.where(
            (slots == s) & same_row, 1.0, 0.0
        ).astype(BF16)
        return carry

    lax.fori_loop(0, 2 * nz, fill, 0)

    h0n.wait_recv()
    h0p.wait_recv()
    pass_on()

    first = (me - 1) * NL

    def nearby(e, k):
        return jnp.clip(nbr_s[e, k] - first, 0, 3 * NL - 1)

    def wait_a(e):
        pltpu.make_async_copy(a_v.at[e], a_v.at[e], a_sem.at[e]).wait()

    def y_copy(s, kind, e, dev):
        return remote(y_out[s].at[kind, e], y_in[s].at[kind, e], y_ss.at[s, kind, e], y_rs.at[s, kind, e], dev)

    def halo_next(st, e):
        return remote(
            xe[st].at[NL + e], xe[st].at[e], halo_ss.at[st - 1, 0, e], halo_rs.at[st - 1, 0, e], nxt
        )

    def halo_prev(st, e):
        return remote(
            xe[st].at[NL + e],
            xe[st].at[2 * NL + e],
            halo_ss.at[st - 1, 1, e],
            halo_rs.at[st - 1, 1, e],
            prv,
        )

    def sides(to_right):
        return (right, rt, left, lt) if to_right else (left, lt, right, rt)

    def gather_right(e, owner):
        return remote(
            xt.at[e], xa.at[e, owner], ag_ss.at[0, e], ag_rs.at[0, e], right
        )

    def gather_left(e, owner):
        return remote(
            xt.at[e], xa.at[e, owner], ag_ss.at[1, e], ag_rs.at[1, e], left
        )

    def gather_on(e, to_right, owner):
        near = sides(to_right)[0]
        return remote(xa.at[e, owner], xa.at[e, owner], ag_ss.at[2, e], ag_rs.at[2, e], near)

    def gather_across(e, owner):
        return remote(xt.at[e], xa.at[e, owner], ag_ss.at[2, e], ag_rs.at[2, e], across)

    def near_of(i):
        return lax.rem(b + 1 + 2 * i, BLK)

    for s in range(SWEEPS):

        def product(e, s=s):
            if s == 0:
                wait_a(e)
            xg[pl.ds(0, RB), :] = xe[s][NL + e]
            for k in range(NBR):
                xg[pl.ds((k + 1) * RB, RB), :] = xe[s][nearby(e, k)]
            y = jnp.dot(a_v[e], xg[...], preferred_element_type=F32)
            ysum[e] = y.reshape(BLK, RB, NC)

        def send_relayed(i, carry, s=s):
            product(i)
            near, far = near_of(i), near_of(i + 1)
            y_out[s][2, i] = ysum[i, op].astype(BF16)
            y_copy(s, 2, i, (me, near)).start()
            y_out[s][1 - i, i] = ysum[i, far].astype(BF16)
            y_copy(s, 1 - i, i, (me, far)).start()
            return carry

        def send_direct(e, carry, s=s):
            product(e)
            for kind, to in ((2, op), (0, rt), (1, lt)):
                y_out[s][kind, e] = ysum[e, to].astype(BF16)
                y_copy(s, kind, e, (me, to)).start()
            return carry

        def relay(i, carry, s=s):
            near = near_of(i)
            y_copy(s, 2, i, (me, near)).wait_recv()
            y_out[s][i, i] = (ysum[i, near] + y_in[s][2, i].astype(F32)).astype(BF16)
            y_copy(s, i, i, (me, near)).start()
            return carry

        lax.fori_loop(0, 2, send_relayed, 0)
        lax.fori_loop(2, NL, send_direct, 0)
        pass_on()
        lax.fori_loop(0, 2, relay, 0)

        def y_sent(e, carry, s=s):
            for kind in range(3):
                y_copy(s, kind, e, right).wait_send()
            return carry

        drains.append(functools.partial(lax.fori_loop, 0, NL, y_sent, 0))

        def update(e, direct, s=s):
            for kind in (0, 1, 2)[: 3 if direct else 2]:
                y_copy(s, kind, e, right).wait_recv()
            y = ysum[e, b] + y_in[s][0, e].astype(F32) + y_in[s][1, e].astype(F32)
            if direct:
                y = y + y_in[s][2, e].astype(F32)
            new = (xe[s][NL + e].astype(F32) - dmp[e] * y).astype(BF16)
            xe[s + 1][NL + e] = new
            halo_next(s + 1, e).start()
            halo_prev(s + 1, e).start()
            if s == SWEEPS - 1:
                turned = new.astype(F32).T.astype(BF16)
                xt[e] = turned
                gather_right(e, b).start()
                gather_left(e, b).start()
                if not direct:
                    gather_across(e, b).start()
                smooth_ref[e] = new
                xa[e, b] = turned

        def update_relayed(e, carry, update=update):
            update(e, False)
            return carry

        def update_direct(e, carry, update=update):
            update(e, True)
            return carry

        lax.fori_loop(2, NL, update_direct, 0)
        lax.fori_loop(0, 2, update_relayed, 0)
        pass_on()

        def halo_in(e, carry, s=s):
            halo_next(s + 1, e).wait_recv()
            halo_prev(s + 1, e).wait_recv()
            return carry

        lax.fori_loop(0, NL, halo_in, 0)

        def halo_out(e, carry, s=s):
            halo_next(s + 1, e).wait_send()
            halo_prev(s + 1, e).wait_send()
            if s == SWEEPS - 1:
                gather_right(e, b).wait_send()
                gather_left(e, b).wait_send()
            return carry

        drains.append(functools.partial(lax.fori_loop, 0, NL, halo_out, 0))
        pass_on()
    gather_right(2, lt).wait_recv()
    gather_on(2, True, lt).start()
    gather_left(3, rt).wait_recv()
    gather_on(3, False, rt).start()
    for e in range(2):
        drains.append(gather_across(e, b).wait_send)
    drains.append(gather_on(2, True, lt).wait_send)
    drains.append(gather_on(3, False, rt).wait_send)

    def couple(e, carry):
        own = me * NL + e
        own_agg = agg_s[own]
        own_grp = grp_s[own_agg]
        x_own = xe[SWEEPS][NL + e]
        xg2[pl.ds(0, RB), pl.ds(0, NC)] = x_own
        xg2[pl.ds(0, RB), pl.ds(NC, NC)] = x_own
        for k in range(NBR):
            near_agg = agg_s[nbr_s[e, k]]
            near_grp = grp_s[near_agg]
            x_near = xe[SWEEPS][nearby(e, k)].astype(F32)
            in_agg = jnp.where(near_agg == own_agg, 1.0, 0.0).astype(F32)
            in_grp = jnp.where(near_grp == own_grp, 1.0, 0.0).astype(F32)
            xg2[pl.ds((k + 1) * RB, RB), pl.ds(0, NC)] = (x_near * in_agg).astype(BF16)
            xg2[pl.ds((k + 1) * RB, RB), pl.ds(NC, NC)] = (x_near * in_grp).astype(BF16)
        zs[e] = jnp.dot(a_v[e], xg2[...], preferred_element_type=F32).astype(BF16)
        return carry

    lax.fori_loop(0, NL, couple, 0)
    pass_on()

    def contract(e, carry):
        gather_across(e, op).wait_recv()
        rows = jnp.concatenate([xa[e, r] for r in range(BLK)], axis=1)
        both = jnp.dot(rows, zs[e], preferred_element_type=F32)
        g_out[:, e] = both[:, :NC].astype(BF16).reshape(BLK, HR, NC)
        h_part[e] = both[:, NC:]
        return carry

    for e in range(NL):
        if e != 3:
            gather_left(e, rt).wait_recv()
        if e != 2:
            gather_right(e, lt).wait_recv()
    lax.fori_loop(0, NL, contract, 0)

    def g_copy(kind, to):
        return remote(g_out.at[to], g_in.at[kind], g_ss.at[kind], g_rs.at[kind], (me, to))

    for kind, to in ((2, op), (0, rt), (1, lt)):
        g_copy(kind, to).start()
        drains.append(g_copy(kind, to).wait_send)

    groups = [grp_s[agg_s[me * NL + e]] for e in range(NL)]

    def group_sum(g, carry):
        acc = jnp.zeros((NC, NC), F32)
        for e in range(NL):
            acc = acc + jnp.where(groups[e] == g, 1.0, 0.0).astype(F32) * h_part[e]
        h_out[g] = acc.astype(BF16).reshape(BLK, HR, NC)
        return carry

    lax.fori_loop(0, 2 * NX, group_sum, 0)
    pl.semaphore_wait(side_sem, 3)

    def h_copy(dx, dc, dy):
        x, c, y = lax.rem(xc + dx, NX), lax.rem(core + dc, 2), lax.rem(b + dy, BLK)
        i = (dx * 2 + dc) * BLK + dy - 1
        dev = ((x * nz + zc) * 2 + c, y)
        return remote(h_out.at[2 * x + c, y], hx.at[(2 * xc + core) * BLK + b], h_ss.at[i], h_rs.at[i], dev)

    def h_arrival(dx, dc, dy):
        x, c, y = lax.rem(xc + NX - dx, NX), lax.rem(core + dc, 2), lax.rem(b + BLK - dy, BLK)
        i = (dx * 2 + dc) * BLK + dy - 1
        return remote(h_out.at[0, 0], hx.at[(2 * x + c) * BLK + y], h_ss.at[i], h_rs.at[i], right)

    others = [
        (dx, dc, dy)
        for dx in (2, 1, 3, 0)
        for dy in (2, 1, 3, 0)
        for dc in (1, 0)
        if dx or dc or dy
    ]
    for o in others:
        h_copy(*o).start()
        drains.append(h_copy(*o).wait_send)
    hx[(2 * xc + core) * BLK + b] = h_out[2 * xc + core, b]

    acc = g_out[b].astype(F32)
    for kind in (0, 1, 2):
        g_copy(kind, rt).wait_recv()
        acc = acc + g_in[kind].astype(F32)
    gx[2 * xc + core] = acc.astype(BF16)

    def x_g(i, owner):
        return remote(gx.at[owner], gx.at[owner], x_ss.at[i], x_rs.at[i], line[i])

    def line_owner(i):
        k = i + 1
        return 2 * lax.rem(xc + NX - k // 2, NX) + lax.rem(core + k % 2, 2)

    for i in (3, 4, 1, 2, 5, 6, 0):
        x_g(i, 2 * xc + core).start()
        drains.append(x_g(i, 2 * xc + core).wait_send)
    zh, zl = zc // zl_n, lax.rem(zc, zl_n)

    def l1_copy(d, owner):
        dev = at(xc, zh * zl_n + lax.rem(zl + d, zl_n), core)
        return remote(l1.at[owner], l1.at[owner], l1_ss.at[d - 1], l1_rs.at[d - 1], dev)

    def l2_copy(d, owner):
        dev = at(xc, lax.rem(zh + d, zh_n) * zl_n + zl, core)
        return remote(l2.at[owner], l2.at[owner], l2_ss.at[d - 1], l2_rs.at[d - 1], dev)

    def summed(ref, n):
        acc = ref[0].astype(F32)
        for i in range(1, n):
            acc = acc + ref[i].astype(F32)
        return acc

    for o in others:
        h_arrival(*o).wait_recv()
    l1[zl] = summed(hx, 2 * NX * BLK).astype(BF16)
    for d in range(1, zl_n):
        l1_copy(d, zl).start()
        drains.append(l1_copy(d, zl).wait_send)

    for i in range(len(line)):
        x_g(i, line_owner(i)).wait_recv()
    for h in range(HR // 16):
        part = gx[:, :, h * 16 : (h + 1) * 16, :].reshape(512, NC)
        sums = jnp.dot(km[...], part, preferred_element_type=F32)
        pb[:, h * 16 : (h + 1) * 16, :] = sums.reshape(2 * nz, 16, NC).astype(BF16)

    def chunk(d):
        return pb.at[pl.ds(lax.rem(zc + nz + d, nz) * 2, 2)]

    def place_z(d):
        return at(xc, lax.rem(zc + nz + d, nz), core)

    eight = (1 - 2 * core) * 4

    def z_far(side, k):
        i = side * 3 + k - 1
        d = (1 - 2 * side) * k
        return remote(
            chunk((1 - 2 * side) * (k + 4)), rfar.at[side, k - 1], z_ss.at[i], z_rs.at[i], place_z(d)
        )

    def z_eight():
        return remote(chunk(8), rz.at[6], z_ss.at[6], z_rs.at[6], place_z(eight))

    def z_near(side, k):
        i = side * 3 + k - 1
        d = (1 - 2 * side) * k
        return remote(chunk(d), rz.at[i], z_ss.at[7 + i], z_rs.at[7 + i], place_z(d))

    def z_last(side):
        d = (1 - 2 * side) * 4
        return remote(four.at[side], rz.at[7 + side], z_ss.at[13 + side], z_rs.at[13 + side], place_z(d))

    for d in range(1, zl_n):
        l1_copy(d, lax.rem(zl + zl_n - d, zl_n)).wait_recv()
    l2[zh] = summed(l1, zl_n).astype(BF16)
    for d in range(1, zh_n):
        l2_copy(d, zh).start()

    z_eight().start()
    drains.append(z_eight().wait_send)
    for k in (3, 2, 1):
        for side in range(2):
            z_far(side, k).start()
            drains.append(z_far(side, k).wait_send)
    for k in (3, 2, 1):
        for side in range(2):
            z_near(side, k).start()
            drains.append(z_near(side, k).wait_send)

    finish()
    sums = [chunk(4 - 8 * side)[...].astype(F32) for side in range(2)]
    for side in range(2):
        for k in (1, 2, 3):
            z_far(side, k).wait_recv()
            sums[side] = sums[side] + rfar[side, k - 1].astype(F32)
    z_eight().wait_recv()
    passed = rz[6].astype(F32)
    for side in range(2):
        share = jnp.where(core == side, 1.0, 0.0).astype(F32)
        four[side] = (sums[side] + share * passed).astype(BF16)
        z_last(side).start()
    for d in range(1, zh_n):
        l2_copy(d, lax.rem(zh + zh_n - d, zh_n)).wait_recv()
    mine = 2 * xc + core
    ll[mine] = summed(l2, zh_n).astype(BF16)

    def final_copy(i, owner):
        return remote(ll.at[owner], ll.at[owner], f_ss.at[i], f_rs.at[i], line[i])

    for i in range(len(line)):
        final_copy(i, mine).start()

    total = pb[pl.ds(zc * 2, 2)].astype(F32)
    for side in range(2):
        for k in (1, 2, 3):
            z_near(side, k).wait_recv()
            total = total + rz[side * 3 + k - 1].astype(F32)
    for side in range(2):
        z_last(side).wait_recv()
        total = total + rz[7 + side].astype(F32)
    coarse_ref[...] = total
    for side in range(2):
        z_last(side).wait_send()
    for d in range(1, zh_n):
        l2_copy(d, zh).wait_send()

    for i in range(len(line)):
        final_copy(i, line_owner(i)).wait_recv()
    last_ref[...] = ll[...].astype(F32)
    for i in range(len(line)):
        final_copy(i, mine).wait_send()


def write_out(a, b, c, a_out, b_out, c_out, a_v, b_v, c_v, in_sem, out_sem):
    held = ((a, a_v, a_out), (b, b_v, b_out), (c, c_v, c_out))
    reads = [pltpu.make_async_copy(x, v, in_sem.at[i]) for i, (x, v, _) in enumerate(held)]
    writes = [pltpu.make_async_copy(v, o, out_sem.at[i]) for i, (_, v, o) in enumerate(held)]
    for read in reads:
        read.start()
    for read, write in zip(reads, writes):
        read.wait()
        write.start()
    for write in writes:
        write.wait()


def body(nz, diag, nbrs, neighbours, damping, bases, agglomerate, group):
    vmem = pl.BlockSpec(memory_space=pltpu.VMEM)
    hbm = pl.BlockSpec(memory_space=pltpu.HBM)
    zl_n = min(4, nz)
    dma = pltpu.SemaphoreType.DMA
    regular = pltpu.SemaphoreType.REGULAR
    V = pltpu.VMEM
    scratch = [
        pltpu.SMEM((NL, NBR), jnp.int32),
        pltpu.SMEM(agglomerate.shape, jnp.int32),
        pltpu.SMEM(group.shape, jnp.int32),
        V((NL, RB), F32),
        V((NL, ROWS, KK), BF16),
        *[V((3 * NL, RB, NC), BF16) for _ in range(SWEEPS + 1)],
        V((KK, NC), BF16),
        V((KK, 2 * NC), BF16),
        V((NL, RB, NC), F32),
        V((NL, BLK, RB, NC), F32),
        *[V((3, NL, RB, NC), BF16) for _ in range(4)],
        V((NL, RB, NC), BF16),
        V((NL, BLK, RB, NC), BF16),
        V((NL, ROWS, 2 * NC), BF16),
        V((NL, NC, NC), F32),
        V((2 * NX, BLK, HR, NC), BF16),
        V((BLK, NL, HR, NC), BF16),
        V((3, NL, HR, NC), BF16),
        V((2 * NX, NL, HR, NC), BF16),
        V((2 * NX * BLK, HR, NC), BF16),
        V((2 * nz * 16, 512), BF16),
        V((2 * nz, HR, NC), BF16),
        V((9, 2, HR, NC), BF16),
        V((2, 3, 2, HR, NC), BF16),
        V((2, 2, HR, NC), BF16),
        V((zl_n, HR, NC), BF16),
        V((nz // zl_n, HR, NC), BF16),
        V((8, HR, NC), BF16),
        dma((5,)),
        dma((NL,)),
        regular,
        regular,
        regular,
        dma((2,)),
        dma((2,)),
        dma((SWEEPS, 2, NL)),
        dma((SWEEPS, 2, NL)),
        dma((SWEEPS, 3, NL)),
        dma((SWEEPS, 3, NL)),
        dma((3, NL)),
        dma((3, NL)),
        dma((2 * NX * BLK - 1,)),
        dma((2 * NX * BLK - 1,)),
        dma((3,)),
        dma((3,)),
        dma((2 * NX - 1,)),
        dma((2 * NX - 1,)),
        dma((nz - 1,)),
        dma((nz - 1,)),
        dma((3,)),
        dma((3,)),
        dma((3,)),
        dma((3,)),
        dma((2 * NX - 1,)),
        dma((2 * NX - 1,)),
    ]
    out = pl.pallas_call(
        functools.partial(kernel, nz),
        out_shape=(
            jax.ShapeDtypeStruct((NL, RB, NC), BF16),
            jax.ShapeDtypeStruct((2, HR, NC), F32),
            jax.ShapeDtypeStruct((8, HR, NC), F32),
        ),
        in_specs=[hbm] * 7,
        out_specs=(vmem, vmem, vmem),
        scratch_shapes=scratch,
        compiler_params=pltpu.CompilerParams(
            collective_id=0, has_side_effects=True, vmem_limit_bytes=LIMIT
        ),
        name="galerkin",
    )(neighbours, agglomerate, group, damping, diag, nbrs, bases)
    return pl.pallas_call(
        write_out,
        out_shape=tuple(jax.ShapeDtypeStruct(o.shape, o.dtype) for o in out),
        in_specs=[hbm] * 3,
        out_specs=(hbm,) * 3,
        scratch_shapes=[*[V(o.shape, o.dtype) for o in out], dma((3,)), dma((3,))],
        compiler_params=pltpu.CompilerParams(vmem_limit_bytes=LIMIT),
        name="write_out",
    )(*out)


def solution(mesh):
    nz = mesh.shape["elem"] // (2 * NX)
    return jax.shard_map(
        functools.partial(body, nz),
        mesh=mesh,
        in_specs=(
            P("elem", None, "blk"),
            P("elem", None, None, "blk"),
            P("elem", None),
            P("elem", "blk"),
            P("elem", "blk", None),
            P(),
            P(),
        ),
        out_specs=(P("elem", "blk", None), P("elem", "blk", None), P(None, "blk", None)),
        check_vma=False,
    )
```

```python
import functools

import jax
import jax.numpy as jnp
from jax import lax
from jax.experimental import pallas as pl
from jax.experimental.pallas import tpu as pltpu
from jax.sharding import PartitionSpec as P

MESH = pl.DeviceIdType.MESH
F32 = jnp.float32
BF16 = jnp.bfloat16
NL = 4
NBR = 6
BLK = 4
NX = 4
NC = 128
RB = 128
ROWS = RB * BLK
KK = (NBR + 1) * RB
HR = NC // BLK
SWEEPS = 2
LIMIT = 62 * 1024 * 1024


def remote(src, dst, send_sem, recv_sem, device):
    return pltpu.make_async_remote_copy(
        src_ref=src,
        dst_ref=dst,
        send_sem=send_sem,
        recv_sem=recv_sem,
        device_id=device,
        device_id_type=MESH,
    )


def kernel(
    nz,
    nbr_h,
    agg_h,
    grp_h,
    damp_h,
    diag_hbm,
    nbrs_hbm,
    bases_hbm,
    smooth_ref,
    coarse_ref,
    last_ref,
    nbr_s,
    agg_s,
    grp_s,
    damp_v,
    a_v,
    xe0,
    xe1,
    xe2,
    xg,
    xg2,
    dmp,
    ysum,
    y_out0,
    y_out1,
    y_in0,
    y_in1,
    xt,
    xa,
    zs,
    h_part,
    h_out,
    g_out,
    g_in,
    gx,
    hx,
    km,
    pb,
    rz,
    rfar,
    four,
    l1,
    l2,
    ll,
    s_sem,
    a_sem,
    up_sem,
    down_sem,
    side_sem,
    halo0_ss,
    halo0_rs,
    halo_ss,
    halo_rs,
    y_ss,
    y_rs,
    ag_ss,
    ag_rs,
    h_ss,
    h_rs,
    g_ss,
    g_rs,
    x_ss,
    x_rs,
    z_ss,
    z_rs,
    l1_ss,
    l1_rs,
    l2_ss,
    l2_rs,
    f_ss,
    f_rs,
):
    xe = (xe0, xe1, xe2)
    y_out = (y_out0, y_out1)
    y_in = (y_in0, y_in1)
    ne = nz * NX * 2
    zl_n = min(4, nz)
    zh_n = nz // zl_n
    me = lax.axis_index("elem")
    b = lax.axis_index("blk")
    core = lax.rem(me, 2)
    zc = lax.rem(me // 2, nz)
    xc = me // (2 * nz)
    rt = lax.rem(b + 1, BLK)
    op = lax.rem(b + 2, BLK)
    lt = lax.rem(b + 3, BLK)
    nxt = (lax.rem(me + 1, ne), b)
    prv = (lax.rem(me + ne - 1, ne), b)
    right, left, across = (me, rt), (me, lt), (me, op)

    def at(x, z, c):
        return ((x * nz + z) * 2 + c, b)

    above = at(xc, lax.rem(zc + 1, nz), core)
    below = at(xc, lax.rem(zc + nz - 1, nz), core)
    line = []
    for dx in range(NX):
        for dc in range(2):
            if dx or dc:
                line.append(at(lax.rem(xc + dx, NX), zc, lax.rem(core + dc, 2)))

    drains = []

    def finish():
        for drain in drains:
            drain()
        drains.clear()

    own_in = pltpu.make_async_copy(bases_hbm, xe[0].at[pl.ds(NL, NL)], s_sem.at[0])
    own_in.start()

    barrier = pltpu.get_barrier_semaphore()
    partners = [across, nxt, prv, right, left, above, below, *line]
    for dev in partners:
        pl.semaphore_signal(barrier, inc=1, device_id=dev, device_id_type=MESH)
    small = [
        pltpu.make_async_copy(src, dst, s_sem.at[i + 1])
        for i, (src, dst) in enumerate(
            ((damp_h, damp_v), (nbr_h, nbr_s), (agg_h, agg_s), (grp_h, grp_s))
        )
    ]
    for copy in small:
        copy.start()
    own_in.wait()
    pl.semaphore_wait(barrier, len(partners))

    h0n = remote(xe[0].at[pl.ds(NL, NL)], xe[0].at[pl.ds(0, NL)], halo0_ss.at[0], halo0_rs.at[0], nxt)
    h0p = remote(
        xe[0].at[pl.ds(NL, NL)], xe[0].at[pl.ds(2 * NL, NL)], halo0_ss.at[1], halo0_rs.at[1], prv
    )
    h0n.start()
    h0p.start()
    for dev in (right, left, across):
        pl.semaphore_signal(side_sem, inc=1, device_id=dev, device_id_type=MESH)
    drains.append(h0n.wait_send)
    drains.append(h0p.wait_send)

    def load_a(e, carry):
        pltpu.make_async_copy(
            diag_hbm.at[e], a_v.at[e, :, pl.ds(0, RB)], a_sem.at[e]
        ).start()
        for k in range(NBR):
            pltpu.make_async_copy(
                nbrs_hbm.at[e, k],
                a_v.at[e, :, pl.ds((k + 1) * RB, RB)],
                a_sem.at[e],
            ).start()
        return carry

    lax.fori_loop(0, NL, load_a, 0)

    last_news = nz // 2 - 1
    news = [0]

    def pass_on():
        j = news[0]
        news[0] += 1
        if 1 <= j <= last_news:
            pl.semaphore_wait(up_sem, 1)
            pl.semaphore_wait(down_sem, 1)
        if j < last_news:
            pl.semaphore_signal(up_sem, inc=1, device_id=above, device_id_type=MESH)
            pl.semaphore_signal(down_sem, inc=1, device_id=below, device_id_type=MESH)

    for copy in small:
        copy.wait()
    for e in range(NL):
        dmp[e] = jnp.broadcast_to(damp_v[pl.ds(e, 1), :], (RB, NC)).T

    lane = lax.broadcasted_iota(jnp.int32, (16, 512), 1)
    row = lax.broadcasted_iota(jnp.int32, (16, 512), 0)

    def place(i, slots):
        xx, cc, j = i // 8, lax.rem(i // 4, 2), lax.rem(i, 4)
        a = agg_s[((xx * nz + zc) * 2 + cc) * NL + j]
        dev = a // 2
        mine = (lax.rem(dev, 2) == core) & (dev // (2 * nz) == xc)
        slot = jnp.where(mine, lax.rem(dev // 2, nz) * 2 + lax.rem(a, 2), -1)
        return jnp.where(lane // 16 == i, slot, slots)

    slots = lax.fori_loop(0, 32, place, jnp.full((16, 512), -1, jnp.int32))
    same_row = row == lax.rem(lane, 16)

    def fill(s, carry):
        km[pl.ds(pl.multiple_of(s * 16, 16), 16), :] = jnp.where(
            (slots == s) & same_row, 1.0, 0.0
        ).astype(BF16)
        return carry

    lax.fori_loop(0, 2 * nz, fill, 0)

    h0n.wait_recv()
    h0p.wait_recv()
    pass_on()

    first = (me - 1) * NL

    def nearby(e, k):
        return jnp.clip(nbr_s[e, k] - first, 0, 3 * NL - 1)

    def wait_a(e):
        pltpu.make_async_copy(a_v.at[e], a_v.at[e], a_sem.at[e]).wait()

    def y_copy(s, kind, e, dev):
        return remote(y_out[s].at[kind, e], y_in[s].at[kind, e], y_ss.at[s, kind, e], y_rs.at[s, kind, e], dev)

    def halo_next(st, e):
        return remote(
            xe[st].at[NL + e], xe[st].at[e], halo_ss.at[st - 1, 0, e], halo_rs.at[st - 1, 0, e], nxt
        )

    def halo_prev(st, e):
        return remote(
            xe[st].at[NL + e],
            xe[st].at[2 * NL + e],
            halo_ss.at[st - 1, 1, e],
            halo_rs.at[st - 1, 1, e],
            prv,
        )

    def sides(to_right):
        return (right, rt, left, lt) if to_right else (left, lt, right, rt)

    def gather_right(e, owner):
        return remote(
            xt.at[e], xa.at[e, owner], ag_ss.at[0, e], ag_rs.at[0, e], right
        )

    def gather_left(e, owner):
        return remote(
            xt.at[e], xa.at[e, owner], ag_ss.at[1, e], ag_rs.at[1, e], left
        )

    def gather_on(e, to_right, owner):
        near = sides(to_right)[0]
        return remote(xa.at[e, owner], xa.at[e, owner], ag_ss.at[2, e], ag_rs.at[2, e], near)

    def gather_across(e, owner):
        return remote(xt.at[e], xa.at[e, owner], ag_ss.at[2, e], ag_rs.at[2, e], across)

    def near_of(i):
        return lax.rem(b + 1 + 2 * i, BLK)

    for s in range(SWEEPS):

        def product(e, s=s):
            if s == 0:
                wait_a(e)
            xg[pl.ds(0, RB), :] = xe[s][NL + e]
            for k in range(NBR):
                xg[pl.ds((k + 1) * RB, RB), :] = xe[s][nearby(e, k)]
            y = jnp.dot(a_v[e], xg[...], preferred_element_type=F32)
            ysum[e] = y.reshape(BLK, RB, NC)

        def send_relayed(i, carry, s=s):
            product(i)
            near, far = near_of(i), near_of(i + 1)
            y_out[s][2, i] = ysum[i, op].astype(BF16)
            y_copy(s, 2, i, (me, near)).start()
            y_out[s][1 - i, i] = ysum[i, far].astype(BF16)
            y_copy(s, 1 - i, i, (me, far)).start()
            return carry

        def send_direct(e, carry, s=s):
            product(e)
            for kind, to in ((2, op), (0, rt), (1, lt)):
                y_out[s][kind, e] = ysum[e, to].astype(BF16)
                y_copy(s, kind, e, (me, to)).start()
            return carry

        def relay(i, carry, s=s):
            near = near_of(i)
            y_copy(s, 2, i, (me, near)).wait_recv()
            y_out[s][i, i] = (ysum[i, near] + y_in[s][2, i].astype(F32)).astype(BF16)
            y_copy(s, i, i, (me, near)).start()
            return carry

        lax.fori_loop(0, 2, send_relayed, 0)
        lax.fori_loop(2, NL, send_direct, 0)
        pass_on()
        lax.fori_loop(0, 2, relay, 0)

        def y_sent(e, carry, s=s):
            for kind in range(3):
                y_copy(s, kind, e, right).wait_send()
            return carry

        drains.append(functools.partial(lax.fori_loop, 0, NL, y_sent, 0))

        def update(e, direct, s=s):
            for kind in (0, 1, 2)[: 3 if direct else 2]:
                y_copy(s, kind, e, right).wait_recv()
            y = ysum[e, b] + y_in[s][0, e].astype(F32) + y_in[s][1, e].astype(F32)
            if direct:
                y = y + y_in[s][2, e].astype(F32)
            new = (xe[s][NL + e].astype(F32) - dmp[e] * y).astype(BF16)
            xe[s + 1][NL + e] = new
            halo_next(s + 1, e).start()
            halo_prev(s + 1, e).start()
            if s == SWEEPS - 1:
                turned = new.astype(F32).T.astype(BF16)
                xt[e] = turned
                gather_right(e, b).start()
                gather_left(e, b).start()
                if not direct:
                    gather_across(e, b).start()
                smooth_ref[e] = new
                xa[e, b] = turned

        def update_relayed(e, carry, update=update):
            update(e, False)
            return carry

        def update_direct(e, carry, update=update):
            update(e, True)
            return carry

        lax.fori_loop(2, NL, update_direct, 0)
        lax.fori_loop(0, 2, update_relayed, 0)
        pass_on()

        def halo_in(e, carry, s=s):
            halo_next(s + 1, e).wait_recv()
            halo_prev(s + 1, e).wait_recv()
            return carry

        lax.fori_loop(0, NL, halo_in, 0)

        def halo_out(e, carry, s=s):
            halo_next(s + 1, e).wait_send()
            halo_prev(s + 1, e).wait_send()
            if s == SWEEPS - 1:
                gather_right(e, b).wait_send()
                gather_left(e, b).wait_send()
            return carry

        drains.append(functools.partial(lax.fori_loop, 0, NL, halo_out, 0))
        pass_on()
    gather_right(2, lt).wait_recv()
    gather_on(2, True, lt).start()
    gather_left(3, rt).wait_recv()
    gather_on(3, False, rt).start()
    for e in range(2):
        drains.append(gather_across(e, b).wait_send)
    drains.append(gather_on(2, True, lt).wait_send)
    drains.append(gather_on(3, False, rt).wait_send)

    def couple(e, carry):
        own = me * NL + e
        own_agg = agg_s[own]
        own_grp = grp_s[own_agg]
        x_own = xe[SWEEPS][NL + e]
        xg2[pl.ds(0, RB), pl.ds(0, NC)] = x_own
        xg2[pl.ds(0, RB), pl.ds(NC, NC)] = x_own
        for k in range(NBR):
            near_agg = agg_s[nbr_s[e, k]]
            near_grp = grp_s[near_agg]
            x_near = xe[SWEEPS][nearby(e, k)].astype(F32)
            in_agg = jnp.where(near_agg == own_agg, 1.0, 0.0).astype(F32)
            in_grp = jnp.where(near_grp == own_grp, 1.0, 0.0).astype(F32)
            xg2[pl.ds((k + 1) * RB, RB), pl.ds(0, NC)] = (x_near * in_agg).astype(BF16)
            xg2[pl.ds((k + 1) * RB, RB), pl.ds(NC, NC)] = (x_near * in_grp).astype(BF16)
        zs[e] = jnp.dot(a_v[e], xg2[...], preferred_element_type=F32).astype(BF16)
        return carry

    lax.fori_loop(0, NL, couple, 0)
    pass_on()

    def contract(e, carry):
        gather_across(e, op).wait_recv()
        rows = jnp.concatenate([xa[e, r] for r in range(BLK)], axis=1)
        both = jnp.dot(rows, zs[e], preferred_element_type=F32)
        g_out[:, e] = both[:, :NC].astype(BF16).reshape(BLK, HR, NC)
        h_part[e] = both[:, NC:]
        return carry

    for e in range(NL):
        if e != 3:
            gather_left(e, rt).wait_recv()
        if e != 2:
            gather_right(e, lt).wait_recv()
    lax.fori_loop(0, NL, contract, 0)

    def g_copy(kind, to):
        return remote(g_out.at[to], g_in.at[kind], g_ss.at[kind], g_rs.at[kind], (me, to))

    for kind, to in ((2, op), (0, rt), (1, lt)):
        g_copy(kind, to).start()
        drains.append(g_copy(kind, to).wait_send)

    groups = [grp_s[agg_s[me * NL + e]] for e in range(NL)]

    def group_sum(g, carry):
        acc = jnp.zeros((NC, NC), F32)
        for e in range(NL):
            acc = acc + jnp.where(groups[e] == g, 1.0, 0.0).astype(F32) * h_part[e]
        h_out[g] = acc.astype(BF16).reshape(BLK, HR, NC)
        return carry

    lax.fori_loop(0, 2 * NX, group_sum, 0)
    pl.semaphore_wait(side_sem, 3)

    def h_copy(dx, dc, dy):
        x, c, y = lax.rem(xc + dx, NX), lax.rem(core + dc, 2), lax.rem(b + dy, BLK)
        i = (dx * 2 + dc) * BLK + dy - 1
        dev = ((x * nz + zc) * 2 + c, y)
        return remote(h_out.at[2 * x + c, y], hx.at[(2 * xc + core) * BLK + b], h_ss.at[i], h_rs.at[i], dev)

    def h_arrival(dx, dc, dy):
        x, c, y = lax.rem(xc + NX - dx, NX), lax.rem(core + dc, 2), lax.rem(b + BLK - dy, BLK)
        i = (dx * 2 + dc) * BLK + dy - 1
        return remote(h_out.at[0, 0], hx.at[(2 * x + c) * BLK + y], h_ss.at[i], h_rs.at[i], right)

    others = [
        (dx, dc, dy)
        for dx in (2, 1, 3, 0)
        for dy in (2, 1, 3, 0)
        for dc in (1, 0)
        if dx or dc or dy
    ]
    for o in others:
        h_copy(*o).start()
        drains.append(h_copy(*o).wait_send)
    hx[(2 * xc + core) * BLK + b] = h_out[2 * xc + core, b]

    acc = g_out[b].astype(F32)
    for kind in (0, 1, 2):
        g_copy(kind, rt).wait_recv()
        acc = acc + g_in[kind].astype(F32)
    gx[2 * xc + core] = acc.astype(BF16)

    def x_g(i, owner):
        return remote(gx.at[owner], gx.at[owner], x_ss.at[i], x_rs.at[i], line[i])

    def line_owner(i):
        k = i + 1
        return 2 * lax.rem(xc + NX - k // 2, NX) + lax.rem(core + k % 2, 2)

    for i in (3, 4, 1, 2, 5, 6, 0):
        x_g(i, 2 * xc + core).start()
        drains.append(x_g(i, 2 * xc + core).wait_send)
    zh, zl = zc // zl_n, lax.rem(zc, zl_n)

    def l1_copy(d, owner):
        dev = at(xc, zh * zl_n + lax.rem(zl + d, zl_n), core)
        return remote(l1.at[owner], l1.at[owner], l1_ss.at[d - 1], l1_rs.at[d - 1], dev)

    def l2_copy(d, owner):
        dev = at(xc, lax.rem(zh + d, zh_n) * zl_n + zl, core)
        return remote(l2.at[owner], l2.at[owner], l2_ss.at[d - 1], l2_rs.at[d - 1], dev)

    def summed(ref, n):
        acc = ref[0].astype(F32)
        for i in range(1, n):
            acc = acc + ref[i].astype(F32)
        return acc

    for o in others:
        h_arrival(*o).wait_recv()
    l1[zl] = summed(hx, 2 * NX * BLK).astype(BF16)
    for d in range(1, zl_n):
        l1_copy(d, zl).start()
        drains.append(l1_copy(d, zl).wait_send)

    for d in range(1, zl_n):
        l1_copy(d, lax.rem(zl + zl_n - d, zl_n)).wait_recv()
    l2[zh] = summed(l1, zl_n).astype(BF16)
    for d in range(1, zh_n):
        l2_copy(d, zh).start()
    for i in range(len(line)):
        x_g(i, line_owner(i)).wait_recv()
    for h in range(HR // 16):
        part = gx[:, :, h * 16 : (h + 1) * 16, :].reshape(512, NC)
        sums = jnp.dot(km[...], part, preferred_element_type=F32)
        pb[:, h * 16 : (h + 1) * 16, :] = sums.reshape(2 * nz, 16, NC).astype(BF16)

    def chunk(d):
        return pb.at[pl.ds(lax.rem(zc + nz + d, nz) * 2, 2)]

    def place_z(d):
        return at(xc, lax.rem(zc + nz + d, nz), core)

    eight = (1 - 2 * core) * 4

    def z_far(side, k):
        i = side * 3 + k - 1
        d = (1 - 2 * side) * k
        return remote(
            chunk((1 - 2 * side) * (k + 4)), rfar.at[side, k - 1], z_ss.at[i], z_rs.at[i], place_z(d)
        )

    def z_eight():
        return remote(chunk(8), rz.at[6], z_ss.at[6], z_rs.at[6], place_z(eight))

    def z_near(side, k):
        i = side * 3 + k - 1
        d = (1 - 2 * side) * k
        return remote(chunk(d), rz.at[i], z_ss.at[7 + i], z_rs.at[7 + i], place_z(d))

    def z_last(side):
        d = (1 - 2 * side) * 4
        return remote(four.at[side], rz.at[7 + side], z_ss.at[13 + side], z_rs.at[13 + side], place_z(d))


    z_eight().start()
    drains.append(z_eight().wait_send)
    for k in (3, 2, 1):
        for side in range(2):
            z_far(side, k).start()
            drains.append(z_far(side, k).wait_send)
    for k in (3, 2, 1):
        for side in range(2):
            z_near(side, k).start()
            drains.append(z_near(side, k).wait_send)

    finish()
    sums = [chunk(4 - 8 * side)[...].astype(F32) for side in range(2)]
    for side in range(2):
        for k in (1, 2, 3):
            z_far(side, k).wait_recv()
            sums[side] = sums[side] + rfar[side, k - 1].astype(F32)
    z_eight().wait_recv()
    passed = rz[6].astype(F32)
    for side in range(2):
        share = jnp.where(core == side, 1.0, 0.0).astype(F32)
        four[side] = (sums[side] + share * passed).astype(BF16)
        z_last(side).start()
    for d in range(1, zh_n):
        l2_copy(d, lax.rem(zh + zh_n - d, zh_n)).wait_recv()
    mine = 2 * xc + core
    ll[mine] = summed(l2, zh_n).astype(BF16)

    def final_copy(i, owner):
        return remote(ll.at[owner], ll.at[owner], f_ss.at[i], f_rs.at[i], line[i])

    for i in range(len(line)):
        final_copy(i, mine).start()

    total = pb[pl.ds(zc * 2, 2)].astype(F32)
    for side in range(2):
        for k in (1, 2, 3):
            z_near(side, k).wait_recv()
            total = total + rz[side * 3 + k - 1].astype(F32)
    for side in range(2):
        z_last(side).wait_recv()
        total = total + rz[7 + side].astype(F32)
    coarse_ref[...] = total
    for side in range(2):
        z_last(side).wait_send()
    for d in range(1, zh_n):
        l2_copy(d, zh).wait_send()

    for i in range(len(line)):
        final_copy(i, line_owner(i)).wait_recv()
    last_ref[...] = ll[...].astype(F32)
    for i in range(len(line)):
        final_copy(i, mine).wait_send()


def write_out(a, b, c, a_out, b_out, c_out, a_v, b_v, c_v, in_sem, out_sem):
    held = ((a, a_v, a_out), (b, b_v, b_out), (c, c_v, c_out))
    reads = [pltpu.make_async_copy(x, v, in_sem.at[i]) for i, (x, v, _) in enumerate(held)]
    writes = [pltpu.make_async_copy(v, o, out_sem.at[i]) for i, (_, v, o) in enumerate(held)]
    for read in reads:
        read.start()
    for read, write in zip(reads, writes):
        read.wait()
        write.start()
    for write in writes:
        write.wait()


def body(nz, diag, nbrs, neighbours, damping, bases, agglomerate, group):
    vmem = pl.BlockSpec(memory_space=pltpu.VMEM)
    hbm = pl.BlockSpec(memory_space=pltpu.HBM)
    zl_n = min(4, nz)
    dma = pltpu.SemaphoreType.DMA
    regular = pltpu.SemaphoreType.REGULAR
    V = pltpu.VMEM
    scratch = [
        pltpu.SMEM((NL, NBR), jnp.int32),
        pltpu.SMEM(agglomerate.shape, jnp.int32),
        pltpu.SMEM(group.shape, jnp.int32),
        V((NL, RB), F32),
        V((NL, ROWS, KK), BF16),
        *[V((3 * NL, RB, NC), BF16) for _ in range(SWEEPS + 1)],
        V((KK, NC), BF16),
        V((KK, 2 * NC), BF16),
        V((NL, RB, NC), F32),
        V((NL, BLK, RB, NC), F32),
        *[V((3, NL, RB, NC), BF16) for _ in range(4)],
        V((NL, RB, NC), BF16),
        V((NL, BLK, RB, NC), BF16),
        V((NL, ROWS, 2 * NC), BF16),
        V((NL, NC, NC), F32),
        V((2 * NX, BLK, HR, NC), BF16),
        V((BLK, NL, HR, NC), BF16),
        V((3, NL, HR, NC), BF16),
        V((2 * NX, NL, HR, NC), BF16),
        V((2 * NX * BLK, HR, NC), BF16),
        V((2 * nz * 16, 512), BF16),
        V((2 * nz, HR, NC), BF16),
        V((9, 2, HR, NC), BF16),
        V((2, 3, 2, HR, NC), BF16),
        V((2, 2, HR, NC), BF16),
        V((zl_n, HR, NC), BF16),
        V((nz // zl_n, HR, NC), BF16),
        V((8, HR, NC), BF16),
        dma((5,)),
        dma((NL,)),
        regular,
        regular,
        regular,
        dma((2,)),
        dma((2,)),
        dma((SWEEPS, 2, NL)),
        dma((SWEEPS, 2, NL)),
        dma((SWEEPS, 3, NL)),
        dma((SWEEPS, 3, NL)),
        dma((3, NL)),
        dma((3, NL)),
        dma((2 * NX * BLK - 1,)),
        dma((2 * NX * BLK - 1,)),
        dma((3,)),
        dma((3,)),
        dma((2 * NX - 1,)),
        dma((2 * NX - 1,)),
        dma((nz - 1,)),
        dma((nz - 1,)),
        dma((3,)),
        dma((3,)),
        dma((3,)),
        dma((3,)),
        dma((2 * NX - 1,)),
        dma((2 * NX - 1,)),
    ]
    out = pl.pallas_call(
        functools.partial(kernel, nz),
        out_shape=(
            jax.ShapeDtypeStruct((NL, RB, NC), BF16),
            jax.ShapeDtypeStruct((2, HR, NC), F32),
            jax.ShapeDtypeStruct((8, HR, NC), F32),
        ),
        in_specs=[hbm] * 7,
        out_specs=(vmem, vmem, vmem),
        scratch_shapes=scratch,
        compiler_params=pltpu.CompilerParams(
            collective_id=0, has_side_effects=True, vmem_limit_bytes=LIMIT
        ),
        name="galerkin",
    )(neighbours, agglomerate, group, damping, diag, nbrs, bases)
    return pl.pallas_call(
        write_out,
        out_shape=tuple(jax.ShapeDtypeStruct(o.shape, o.dtype) for o in out),
        in_specs=[hbm] * 3,
        out_specs=(hbm,) * 3,
        scratch_shapes=[*[V(o.shape, o.dtype) for o in out], dma((3,)), dma((3,))],
        compiler_params=pltpu.CompilerParams(vmem_limit_bytes=LIMIT),
        name="write_out",
    )(*out)


def solution(mesh):
    nz = mesh.shape["elem"] // (2 * NX)
    return jax.shard_map(
        functools.partial(body, nz),
        mesh=mesh,
        in_specs=(
            P("elem", None, "blk"),
            P("elem", None, None, "blk"),
            P("elem", None),
            P("elem", "blk"),
            P("elem", "blk", None),
            P(),
            P(),
        ),
        out_specs=(P("elem", "blk", None), P("elem", "blk", None), P(None, "blk", None)),
        check_vma=False,
    )
```
